32 devices in a mesh: dp: 16 (over z, x, core), tensor: 2 (over y).
Axes of the slice: x: 2, y: 2, z: 4, core: 2. Of those that a mesh axis runs over, the one named last changes fastest.
Arguments:
- frames: bfloat16 [4096, 1536], P('dp', 'tensor'), may hold values from -6 to 6
- norm_gain: float32 [1536], replicated, may hold values from 0.5 to 2
- norm_bias: float32 [1536], replicated, may hold values from -3 to 3
- input_weight: bfloat16 [2, 1536, 1536], P(None, 'tensor'), may hold values from -0.15625 to 0.15625
- depth_weight: float32 [32, 1536], P(None, 'tensor'), may hold values from -1.5 to 1.5
- batch_scale: float32 [1536], P('tensor'), may hold values from 0.5 to 2
- batch_shift: float32 [1536], P('tensor'), may hold values from -3 to 3
- output_weight: bfloat16 [1536, 1536], P('tensor'), may hold values from -0.15625 to 0.15625
- upstream: bfloat16 [8192, 1536], P(('dp', 'tensor')), may hold values from -6 to 6
- replica_blocks: int32 [16], replicated, may hold values from 0 to 64, as said below
- segment: int32 [8192], P('dp'), may hold values from 0 to 32, as said below
Outputs:
- block_output: bfloat16 [8192, 1536], P(('dp', 'tensor'))
- frame_gradient: bfloat16 [4096, 1536], P('dp', 'tensor')
- input_weight_gradient: bfloat16 [2, 1536, 1536], P(None, 'tensor')
- output_weight_gradient: bfloat16 [1536, 1536], P('tensor')
- depth_weight_gradient: float32 [32, 1536], P(None, 'tensor')
- gain_gradient: float32 [1536], P('tensor')
- bias_gradient: float32 [1536], P('tensor')
The draws below stay inside these ranges and needn't reach their ends.
Inputs may be any that keep to these rules, and one draw needn't show every extreme that they name: `replica_blocks`: the counts sum to 512. `segment`: within a replica's 512 slots the number starts at 0 and never falls.
All inputs are finite; a program needn't handle non-finite values.
Results may differ from the reference program's by a relative error of at most 0.017.
Values may be sent and summed in bfloat16 or wider, within the bound.
A program may use at most 128 MiB of HBM per device.

```python
import math
import jax
import jax.numpy as jnp
from jax import lax

D = 1536
KERNEL = 32
BLK = 8
LOAD_DEV = 256
FR_DEV = 512
LOADED = 4096
TOKENS = 8192
N_DP = 16
N_TENSOR = 2


def draw_replica_blocks(key, part):
    key = jax.random.fold_in(key, 11)
    perm_key, move_key = jax.random.split(key)
    load_blocks = LOAD_DEV // BLK
    order = jax.random.permutation(perm_key, N_DP).astype(jnp.int32)
    moved = jax.random.randint(move_key, (N_DP // 2,), 0, load_blocks + 1).astype(jnp.int32)
    moved = moved.at[0].set(load_blocks)
    counts = jnp.zeros((N_DP,), jnp.int32)
    counts = counts.at[order[0::2]].set(load_blocks + moved)
    counts = counts.at[order[1::2]].set(load_blocks - moved)
    return counts


def draw_segment(key, part):
    key = jax.random.fold_in(key, 23)
    marks = (jax.random.randint(key, (N_DP, FR_DEV), 0, 64) == 0).astype(jnp.int32)
    every_eighth = (jnp.arange(FR_DEV, dtype=jnp.int32) % 8 == 0).astype(jnp.int32)
    marks = marks.at[0].set(jnp.maximum(marks[0], every_eighth))
    marks = marks.at[:, 0].set(0)
    counted = jnp.cumsum(marks, axis=1).astype(jnp.int32)
    return jnp.minimum(counted, FR_DEV // 16).astype(jnp.int32).reshape(-1)


def levels(own_key, extent, cuts, smallest, top_value):
    def one(axis_at, blocks):
        heights = jax.random.uniform(jax.random.fold_in(jax.random.fold_in(own_key, 6), axis_at), (blocks,), jnp.float32, smallest / len(cuts), top_value / len(cuts))
        return jnp.repeat(jnp.exp(heights), extent[axis_at] // blocks).reshape((-1,) + (1,) * (len(extent) - axis_at - 1))

    factor_of = one(*cuts[0])
    for cut in cuts[1:]:
        factor_of = factor_of * one(*cut)
    return factor_of


def noise(stream_key, shape, scale, limit, shards=(), kind=jnp.bfloat16):
    loudness = levels(stream_key, shape, shards, -0.22, 0.18) if shards else 1.0
    drawn = jax.random.normal(stream_key, shape, jnp.float32) * scale * loudness
    return jnp.minimum(jnp.maximum(drawn, -limit), limit).astype(kind)


def setup_inputs(seed: int = 0) -> dict:
    key_of = jax.random.split(jax.random.key(seed), 12)
    return {
        "frames": noise(key_of[0], (LOADED, D), 1.0, 6.0, ((0, 16), (1, 2))),
        "norm_gain": jnp.clip(jnp.exp(jax.random.uniform(key_of[1], (D,), jnp.float32, math.log(0.5), math.log(2.0))), 0.5, 2.0),
        "norm_bias": noise(key_of[2], (D,), 0.5, 3.0, (), jnp.float32),
        "input_weight": noise(key_of[3], (2, D, D), D ** -0.5, 0.15625, ((1, 2),)),
        "depth_weight": noise(key_of[4], (KERNEL, D), (KERNEL // 2) ** -0.5, 1.5, ((1, 2),), jnp.float32),
        "batch_scale": jnp.clip(jnp.exp(math.log(2.0) - 1.3862944 * jax.random.uniform(key_of[5], (D,), jnp.float32) ** levels(key_of[5], (D,), ((0, 2),), -0.2, 0.2)), 0.5, 2.0),
        "batch_shift": noise(key_of[6], (D,), 0.5, 3.0, ((0, 2),), jnp.float32),
        "output_weight": noise(key_of[7], (D, D), D ** -0.5, 0.15625, ((0, 2),)),
        "upstream": noise(key_of[8], (TOKENS, D), 1.0, 6.0, ((0, 32),)),
        "replica_blocks": draw_replica_blocks(jax.random.fold_in(key_of[11], 71), 0),
        "segment": draw_segment(jax.random.fold_in(key_of[11], 71), 0),
    }


epsilon = 1e-05

def rounded(value):
    return lax.optimization_barrier(value.astype(jnp.bfloat16)).astype(jnp.float32)

def reference(frames, norm_gain, norm_bias, input_weight, depth_weight, batch_scale, batch_shift, output_weight, upstream, replica_blocks, segment):
    load_blocks = LOAD_DEV // BLK
    cap_blocks = 2 * load_blocks
    row_count = FR_DEV
    group = D // N_TENSOR
    run_ends = jnp.cumsum(replica_blocks).astype(jnp.int32)
    starts = (run_ends - replica_blocks).astype(jnp.int32)
    numbers = jnp.arange(N_DP * load_blocks, dtype=jnp.int32)
    loader = numbers % N_DP
    turn = numbers // N_DP
    target = lax.optimization_barrier(jnp.sum((run_ends[None, :] <= numbers[:, None]).astype(jnp.int32), axis=1)).astype(jnp.int32)
    position = numbers - starts[target]
    source_block = (loader * load_blocks + turn).astype(jnp.int32)
    slot_block = (target * cap_blocks + position).astype(jnp.int32)
    block_view = frames.reshape(N_DP * load_blocks, BLK, D)
    packed = jnp.zeros((N_DP * cap_blocks, BLK, D), jnp.bfloat16).at[slot_block].set(block_view[source_block])
    x_rows = packed.reshape(N_DP, row_count, D)
    active = (jnp.arange(row_count, dtype=jnp.int32) // BLK)[None, :] < replica_blocks[:, None]
    seg_rows = segment.reshape(N_DP, row_count)
    x_float = x_rows.astype(jnp.float32)
    center = lax.optimization_barrier(jnp.mean(x_float, axis=-1, keepdims=True))
    spread = lax.optimization_barrier(jnp.mean(jnp.square(x_float - center), axis=-1, keepdims=True))
    scale_row = lax.rsqrt(spread + epsilon)
    standard = (x_float - center) * scale_row
    normed = (standard * norm_gain + norm_bias).astype(jnp.bfloat16)
    flat_normed = normed.reshape(-1, D)
    linear = jnp.dot(flat_normed, input_weight[0].T, preferred_element_type=jnp.float32).reshape(N_DP, row_count, D)
    gate = jnp.dot(flat_normed, input_weight[1].T, preferred_element_type=jnp.float32).reshape(N_DP, row_count, D)
    gate_sigmoid = jax.nn.sigmoid(gate)
    glu = (linear * gate_sigmoid).astype(jnp.bfloat16)
    front = KERNEL // 2
    back = KERNEL - 1 - front
    seg_pad = jnp.pad(seg_rows, ((0, 0), (front, back)), constant_values=-1)
    active_pad = jnp.pad(active, ((0, 0), (front, back)))
    glu_pad = jnp.pad(glu, ((0, 0), (front, back), (0, 0)))
    tap_masks = []
    for offset in range(KERNEL):
        same = (seg_pad[:, offset:offset + row_count] == seg_rows) & active_pad[:, offset:offset + row_count]
        tap_masks.append(same.astype(jnp.float32)[:, :, None])
    conv_sum = jnp.zeros((N_DP, row_count, D), jnp.float32)
    for offset in range(KERNEL):
        conv_sum = conv_sum + depth_weight[offset] * glu_pad[:, offset:offset + row_count].astype(jnp.float32) * tap_masks[offset]
    preswish = conv_sum * batch_scale + batch_shift
    pre_sigmoid = jax.nn.sigmoid(preswish)
    swish = (preswish * pre_sigmoid).astype(jnp.bfloat16)
    flat_swish = swish.reshape(-1, D)
    mixed_sum = jnp.zeros((N_DP * row_count, D), jnp.float32)
    for index in range(N_TENSOR):
        lower = index * group
        term = jnp.dot(flat_swish[:, lower:lower + group], output_weight[lower:lower + group], preferred_element_type=jnp.float32)
        mixed_sum = mixed_sum + rounded(term)
    mixed_sum = mixed_sum.reshape(N_DP, row_count, D)
    active_col = active[:, :, None]
    block_output = jnp.where(active_col, x_float + mixed_sum, 0.0).astype(jnp.bfloat16)
    cotangent = upstream.reshape(N_DP, row_count, D)
    delta_out = jnp.where(active_col, cotangent, jnp.zeros_like(cotangent))
    flat_delta = delta_out.reshape(-1, D)
    delta_swish = jnp.dot(flat_delta, output_weight.T, preferred_element_type=jnp.float32).reshape(N_DP, row_count, D)
    output_weight_gradient = jnp.dot(flat_swish.T, flat_delta, preferred_element_type=jnp.float32).astype(jnp.bfloat16)
    delta_conv = delta_swish * pre_sigmoid * (1.0 + preswish * (1.0 - pre_sigmoid)) * batch_scale
    delta_pad = jnp.zeros((N_DP, row_count + KERNEL - 1, D), jnp.float32)
    tap_rows = []
    for offset in range(KERNEL):
        contrib = delta_conv * tap_masks[offset]
        delta_pad = delta_pad.at[:, offset:offset + row_count].add(depth_weight[offset] * contrib)
        tap_rows.append(lax.optimization_barrier(jnp.sum(contrib * glu_pad[:, offset:offset + row_count].astype(jnp.float32), axis=(0, 1))))
    delta_glu = delta_pad[:, front:front + row_count]
    depth_weight_gradient = jnp.stack(tap_rows)
    delta_linear = (delta_glu * gate_sigmoid).astype(jnp.bfloat16).reshape(-1, D)
    delta_gate = (delta_glu * linear * gate_sigmoid * (1.0 - gate_sigmoid)).astype(jnp.bfloat16).reshape(-1, D)
    input_weight_gradient = jnp.stack([jnp.dot(delta_linear.T, flat_normed, preferred_element_type=jnp.float32), jnp.dot(delta_gate.T, flat_normed, preferred_element_type=jnp.float32)]).astype(jnp.bfloat16)
    delta_normed = jnp.zeros((N_DP * row_count, D), jnp.float32)
    for index in range(N_TENSOR):
        lower = index * group
        term = jnp.dot(delta_linear[:, lower:lower + group], input_weight[0][lower:lower + group], preferred_element_type=jnp.float32)
        term = term + jnp.dot(delta_gate[:, lower:lower + group], input_weight[1][lower:lower + group], preferred_element_type=jnp.float32)
        delta_normed = delta_normed + rounded(term)
    delta_normed = delta_normed.reshape(N_DP, row_count, D)
    gain_gradient = lax.optimization_barrier(jnp.sum(delta_normed * standard, axis=(0, 1)))
    bias_gradient = lax.optimization_barrier(jnp.sum(delta_normed, axis=(0, 1)))
    delta_standard = delta_normed * norm_gain
    delta_x = delta_out.astype(jnp.float32) + scale_row * (delta_standard - lax.optimization_barrier(jnp.mean(delta_standard, axis=-1, keepdims=True)) - standard * lax.optimization_barrier(jnp.mean(delta_standard * standard, axis=-1, keepdims=True)))
    delta_blocks = delta_x.astype(jnp.bfloat16).reshape(N_DP * cap_blocks, BLK, D)
    frame_gradient = jnp.zeros((N_DP * load_blocks, BLK, D), jnp.bfloat16).at[source_block].set(delta_blocks[slot_block]).reshape(N_DP * LOAD_DEV, D)
    return (block_output.reshape(N_DP * row_count, D), frame_gradient, input_weight_gradient, output_weight_gradient, depth_weight_gradient, gain_gradient, bias_gradient)
```

```python
import functools

import jax
import jax.numpy as jnp
from jax import lax
from jax.experimental import pallas as pl
from jax.experimental.pallas import tpu as pltpu
from jax.sharding import PartitionSpec as P

BLK = 8


epsilon = 1e-05


def cdiv(a, b):
    return (a + b - 1) // b


def conv_kernel(
    taps,
    front,
    tile,
    linear_ref,
    gate_ref,
    delta_ref,
    seg_ref,
    active_ref,
    weight_ref,
    scale_ref,
    shift_ref,
    swish_ref,
    dlin_ref,
    dgate_ref,
    tap_ref,
    glu_pad,
    conv_pad,
    seg_pad,
    tap_acc,
):
    rows, width = linear_ref.shape
    pad = taps
    padded = rows + 2 * pad

    zeros = jnp.zeros((pad, width), jnp.float32)
    glu_pad[0:pad, :] = zeros
    glu_pad[pad + rows : padded, :] = zeros
    conv_pad[0:pad, :] = zeros
    conv_pad[pad + rows : padded, :] = zeros

    @pl.when(pl.program_id(0) == 0)
    def _():
        outside = jnp.full((pad, width), -1, jnp.int32)
        seg_pad[0:pad, :] = outside
        seg_pad[pad + rows : padded, :] = outside
        seg_pad[pad : pad + rows, :] = jnp.broadcast_to(seg_ref[...], (rows, width))

    tap_acc[...] = jnp.zeros_like(tap_acc)

    for start in range(0, rows, tile):
        part = pl.ds(start, tile)
        glu = linear_ref[part, :] * jax.nn.sigmoid(gate_ref[part, :])
        glu = glu.astype(jnp.bfloat16).astype(jnp.float32)
        glu_pad[pl.ds(pad + start, tile), :] = jnp.where(active_ref[part, :] > 0, glu, 0.0)

    @pl.loop(0, rows // tile)
    def _(step):
        start = pl.multiple_of(step * tile, tile)
        part = pl.ds(start, tile)
        own = seg_pad[pl.ds(pad + start, tile), :]
        total = jnp.zeros((tile, width), jnp.float32)
        for j in range(taps):
            near = pl.ds(start + (pad + j - front), tile)
            picked = jnp.where(seg_pad[near, :] == own, glu_pad[near, :], 0.0)
            total = total + weight_ref[j : j + 1, :] * picked
        scale = scale_ref[...]
        preswish = total * scale + shift_ref[...]
        pre_sigmoid = jax.nn.sigmoid(preswish)
        swish_ref[part, :] = (preswish * pre_sigmoid).astype(jnp.bfloat16)
        conv_pad[pl.ds(pad + start, tile), :] = (
            delta_ref[part, :]
            * pre_sigmoid
            * (1.0 + preswish * (1.0 - pre_sigmoid))
            * scale
        )

    @pl.loop(0, rows // tile)
    def _(step):
        start = pl.multiple_of(step * tile, tile)
        part = pl.ds(start, tile)
        own = seg_pad[pl.ds(pad + start, tile), :]
        glu = glu_pad[pl.ds(pad + start, tile), :]
        total = jnp.zeros((tile, width), jnp.float32)
        for j in range(taps):
            near = pl.ds(start + (pad + front - j), tile)
            picked = jnp.where(seg_pad[near, :] == own, conv_pad[near, :], 0.0)
            total = total + weight_ref[j : j + 1, :] * picked
            product = (glu * picked).reshape(tile // 8, 8, width)
            tap_acc[j] = tap_acc[j] + jnp.sum(product, axis=0)
        total = jnp.where(active_ref[part, :] > 0, total, 0.0)
        gate_sigmoid = jax.nn.sigmoid(gate_ref[part, :])
        dlin = total * gate_sigmoid
        dlin_ref[part, :] = dlin.astype(jnp.bfloat16)
        dgate_ref[part, :] = (dlin * linear_ref[part, :] * (1.0 - gate_sigmoid)).astype(
            jnp.bfloat16
        )

    tap_ref[...] = jnp.sum(tap_acc[...], axis=1)


def conv_both(projected, delta_swish, segment, active, weight, scale, shift):
    _, rows, given = projected.shape
    taps = weight.shape[0]
    width = 128
    channels = cdiv(given, width) * width

    def widen(array):
        extra = channels - given
        return jnp.pad(array, [(0, 0)] * (array.ndim - 1) + [(0, extra)]) if extra else array

    projected, delta_swish, weight = widen(projected), widen(delta_swish), widen(weight)
    scale, shift = widen(scale), widen(shift)
    tile = min(64, rows)
    padded = rows + 2 * taps
    column = pl.BlockSpec((rows, width), lambda c: (0, c))
    half = lambda h: pl.BlockSpec((None, rows, width), lambda c: (h, 0, c))
    row = pl.BlockSpec((1, width), lambda c: (0, c))
    whole = pl.BlockSpec((rows, 1), lambda c: (0, 0))
    results = pl.pallas_call(
        functools.partial(conv_kernel, taps, taps // 2, tile),
        grid=(channels // width,),
        out_shape=(
            jax.ShapeDtypeStruct((rows, channels), jnp.bfloat16),
            jax.ShapeDtypeStruct((rows, channels), jnp.bfloat16),
            jax.ShapeDtypeStruct((rows, channels), jnp.bfloat16),
            jax.ShapeDtypeStruct((taps, channels), jnp.float32),
        ),
        in_specs=[
            half(0),
            half(1),
            column,
            whole,
            whole,
            pl.BlockSpec((taps, width), lambda c: (0, c)),
            row,
            row,
        ],
        out_specs=[column, column, column, pl.BlockSpec((taps, width), lambda c: (0, c))],
        scratch_shapes=[
            pltpu.VMEM((padded, width), jnp.float32),
            pltpu.VMEM((padded, width), jnp.float32),
            pltpu.VMEM((padded, width), jnp.int32),
            pltpu.VMEM((taps, 8, width), jnp.float32),
        ],
        compiler_params=pltpu.CompilerParams(vmem_limit_bytes=24 * 1024 * 1024),
        cost_estimate=pl.CostEstimate(
            flops=10 * rows * channels * taps,
            bytes_accessed=18 * rows * channels,
            transcendentals=3 * rows * channels,
        ),
    )(
        projected,
        projected,
        delta_swish,
        segment[:, None],
        active.astype(jnp.int32)[:, None],
        weight,
        scale[None, :],
        shift[None, :],
    )
    return [result[:, :given] for result in results] if channels != given else results


def on_device(
    frames,
    norm_gain,
    norm_bias,
    input_weight,
    depth_weight,
    batch_scale,
    batch_shift,
    output_weight,
    upstream,
    replica_blocks,
    segment,
):
    replicas = lax.axis_size("dp")
    my_index = lax.axis_index("dp")
    tensor_index = lax.axis_index("tensor")
    full_width = norm_gain.shape[0]
    load_rows, part_width = frames.shape
    row_count = segment.shape[0]
    rows_part = upstream.shape[0]
    load_blocks = load_rows // BLK
    cap_blocks = row_count // BLK
    per_peer = cdiv(cap_blocks, replicas)
    row_start = tensor_index * rows_part
    column_start = tensor_index * part_width

    run_ends = jnp.cumsum(replica_blocks)
    starts = run_ends - replica_blocks
    peers = jnp.arange(replicas, dtype=jnp.int32)
    is_mine = peers == my_index
    my_start = jnp.sum(jnp.where(is_mine, starts, 0))
    my_blocks = jnp.sum(jnp.where(is_mine, replica_blocks, 0))
    my_end = my_start + my_blocks
    bucket = jnp.arange(per_peer, dtype=jnp.int32)
    first_out = cdiv(jnp.maximum(starts - my_index, 0), replicas)
    send_block = jnp.minimum(first_out[:, None] + bucket[None, :], load_blocks - 1)
    skipped = cdiv(jnp.maximum(my_start - peers, 0), replicas)
    arriving = peers[:, None] + replicas * (skipped[:, None] + bucket[None, :])
    landing = jnp.clip(arriving - my_start, 0, cap_blocks - 1)
    slots = jnp.arange(cap_blocks, dtype=jnp.int32)
    slot_number = my_start + slots
    slot_source = slot_number % replicas
    slot_skipped = cdiv(jnp.maximum(my_start - slot_source, 0), replicas)
    slot_pos = jnp.clip(slot_number // replicas - slot_skipped, 0, per_peer - 1)
    pick_in = slot_source * per_peer + slot_pos
    load_numbers = my_index + replicas * jnp.arange(load_blocks, dtype=jnp.int32)
    target = jnp.sum((run_ends[None, :] <= load_numbers[:, None]).astype(jnp.int32), axis=1)
    target_start = jnp.sum(jnp.where(peers[None, :] == target[:, None], starts[None, :], 0), axis=1)
    slot_out = jnp.arange(load_blocks, dtype=jnp.int32) - cdiv(
        jnp.maximum(target_start - my_index, 0), replicas
    )
    pick_back = target * per_peer + slot_out

    active = slots < my_blocks
    active_rows = jnp.repeat(active, BLK)
    active_mine = lax.dynamic_slice_in_dim(active_rows, row_start, rows_part)[:, None]

    delta_piece = jnp.where(active_mine, upstream, jnp.zeros_like(upstream))
    delta_whole = lax.all_gather(delta_piece, "tensor", axis=0, tiled=True)

    outbox = frames.reshape(load_blocks, BLK, part_width)[send_block.reshape(-1)]
    arrived = lax.all_to_all(
        outbox.reshape(replicas, per_peer, BLK, part_width),
        "dp",
        split_axis=0,
        concat_axis=0,
        tiled=True,
    )
    packed = jnp.where(
        active[:, None, None],
        arrived.reshape(replicas * per_peer, BLK, part_width)[pick_in],
        jnp.zeros((), jnp.bfloat16),
    )
    local_rows = packed.reshape(row_count, part_width)
    gathered = lax.all_gather(local_rows, "tensor", axis=1, tiled=True)

    delta_swish = lax.dot_general(
        delta_whole, output_weight, (((1,), (1,)), ((), ())), preferred_element_type=jnp.float32
    )

    gathered_float = gathered.astype(jnp.float32)
    center = jnp.mean(gathered_float, axis=1, keepdims=True)
    spread = jnp.mean(jnp.square(gathered_float - center), axis=1, keepdims=True)
    scale_row = lax.rsqrt(spread + epsilon)
    standard_full = (gathered_float - center) * scale_row
    normed = (standard_full * norm_gain + norm_bias).astype(jnp.bfloat16)
    projected = jnp.einsum("td,kcd->ktc", normed, input_weight, preferred_element_type=jnp.float32)

    swish, delta_linear, delta_gate, tap_local = conv_both(
        projected, delta_swish, segment, active_rows, depth_weight, batch_scale, batch_shift
    )

    back_term = (
        jnp.dot(delta_linear, input_weight[0], preferred_element_type=jnp.float32)
        + jnp.dot(delta_gate, input_weight[1], preferred_element_type=jnp.float32)
    ).astype(jnp.bfloat16)
    delta_normed = lax.psum_scatter(back_term, "tensor", scatter_dimension=1, tiled=True).astype(
        jnp.float32
    )
    back_float = back_term.astype(jnp.float32)
    back_standard = back_float * standard_full
    unit_local = jnp.sum(back_float * norm_gain, axis=1)
    cross_local = jnp.sum(back_standard * norm_gain, axis=1)
    unit_total, cross_total = lax.psum((unit_local, cross_local), "tensor")
    norm_sums = lax.psum(
        jnp.stack([jnp.sum(back_standard, axis=0), jnp.sum(back_float, axis=0)]), ("dp", "tensor")
    )
    norm_part = lax.dynamic_slice_in_dim(norm_sums, column_start, part_width, 1)

    mixed_sum = lax.psum_scatter(
        jnp.dot(swish, output_weight, preferred_element_type=jnp.float32).astype(jnp.bfloat16),
        "tensor",
        scatter_dimension=0,
        tiled=True,
    ).astype(jnp.float32)
    residual_part = lax.dynamic_slice_in_dim(gathered, row_start, rows_part, 0)
    block_output = jnp.where(
        active_mine, residual_part.astype(jnp.float32) + mixed_sum, 0.0
    ).astype(jnp.bfloat16)

    def over_rows(left, right):
        return lax.dot_general(
            left, right, (((0,), (0,)), ((), ())), preferred_element_type=jnp.float32
        ).astype(jnp.bfloat16)

    def summed(term):
        piece = lax.psum_scatter(term, "dp", scatter_dimension=0, tiled=True)
        return lax.all_gather(piece, "dp", axis=0, tiled=True)

    out_summed = summed(over_rows(swish, delta_whole))
    linear_summed = summed(over_rows(delta_linear, normed))
    gate_summed = summed(over_rows(delta_gate, normed))
    tap_summed = lax.psum(tap_local, "dp")

    gain_part = lax.dynamic_slice_in_dim(norm_gain, column_start, part_width)
    standard = (local_rows.astype(jnp.float32) - center) * scale_row
    delta_part = lax.dynamic_slice_in_dim(delta_whole, column_start, part_width, 1)
    delta_rows = delta_part.astype(jnp.float32) + scale_row * (
        delta_normed * gain_part
        - (unit_total / full_width)[:, None]
        - standard * (cross_total / full_width)[:, None]
    )
    delta_blocks = delta_rows.astype(jnp.bfloat16).reshape(cap_blocks, BLK, part_width)
    homebound = delta_blocks[landing.reshape(-1)].reshape(replicas, per_peer, BLK, part_width)
    returned = lax.all_to_all(homebound, "dp", split_axis=0, concat_axis=0, tiled=True)
    frame_gradient = returned.reshape(replicas * per_peer, BLK, part_width)[pick_back].reshape(
        load_rows, part_width
    )
    return (
        block_output,
        frame_gradient,
        jnp.stack([linear_summed, gate_summed]),
        out_summed,
        tap_summed,
        norm_part[0],
        norm_part[1],
    )


def solution(mesh):
    in_specs = (
        P("dp", "tensor"),
        P(),
        P(),
        P(None, "tensor", None),
        P(None, "tensor"),
        P("tensor"),
        P("tensor"),
        P("tensor", None),
        P(("dp", "tensor"), None),
        P(),
        P("dp"),
    )
    out_specs = (
        P(("dp", "tensor"), None),
        P("dp", "tensor"),
        P(None, "tensor", None),
        P("tensor", None),
        P(None, "tensor"),
        P("tensor"),
        P("tensor"),
    )
    return jax.shard_map(
        on_device, mesh=mesh, in_specs=in_specs, out_specs=out_specs, check_vma=False
    )
```

```python
import functools

import jax
import jax.numpy as jnp
from jax import lax
from jax.experimental import pallas as pl
from jax.experimental.pallas import tpu as pltpu
from jax.sharding import PartitionSpec as P

BLK = 8


epsilon = 1e-05


def cdiv(a, b):
    return (a + b - 1) // b


def conv_kernel(
    taps,
    front,
    tile,
    linear_ref,
    gate_ref,
    delta_ref,
    seg_ref,
    active_ref,
    weight_ref,
    scale_ref,
    shift_ref,
    swish_ref,
    dlin_ref,
    dgate_ref,
    tap_ref,
    glu_pad,
    conv_pad,
    seg_pad,
    tap_acc,
):
    rows, width = linear_ref.shape
    pad = taps
    padded = rows + 2 * pad

    zeros = jnp.zeros((pad, width), jnp.float32)
    glu_pad[0:pad, :] = zeros
    glu_pad[pad + rows : padded, :] = zeros
    conv_pad[0:pad, :] = zeros
    conv_pad[pad + rows : padded, :] = zeros

    @pl.when(pl.program_id(0) == 0)
    def _():
        outside = jnp.full((pad, width), -1, jnp.int32)
        seg_pad[0:pad, :] = outside
        seg_pad[pad + rows : padded, :] = outside
        seg_pad[pad : pad + rows, :] = jnp.broadcast_to(seg_ref[...], (rows, width))

    tap_acc[...] = jnp.zeros_like(tap_acc)

    for start in range(0, rows, tile):
        part = pl.ds(start, tile)
        glu = linear_ref[part, :] * jax.nn.sigmoid(gate_ref[part, :])
        glu = glu.astype(jnp.bfloat16).astype(jnp.float32)
        glu_pad[pl.ds(pad + start, tile), :] = jnp.where(active_ref[part, :] > 0, glu, 0.0)

    @pl.loop(0, rows // tile)
    def _(step):
        start = pl.multiple_of(step * tile, tile)
        part = pl.ds(start, tile)
        own = seg_pad[pl.ds(pad + start, tile), :]
        total = jnp.zeros((tile, width), jnp.float32)
        for j in range(taps):
            near = pl.ds(start + (pad + j - front), tile)
            picked = jnp.where(seg_pad[near, :] == own, glu_pad[near, :], 0.0)
            total = total + weight_ref[j : j + 1, :] * picked
        scale = scale_ref[...]
        preswish = total * scale + shift_ref[...]
        pre_sigmoid = jax.nn.sigmoid(preswish)
        swish_ref[part, :] = (preswish * pre_sigmoid).astype(jnp.bfloat16)
        conv_pad[pl.ds(pad + start, tile), :] = (
            delta_ref[part, :]
            * pre_sigmoid
            * (1.0 + preswish * (1.0 - pre_sigmoid))
            * scale
        )

    @pl.loop(0, rows // tile)
    def _(step):
        start = pl.multiple_of(step * tile, tile)
        part = pl.ds(start, tile)
        own = seg_pad[pl.ds(pad + start, tile), :]
        glu = glu_pad[pl.ds(pad + start, tile), :]
        total = jnp.zeros((tile, width), jnp.float32)
        for j in range(taps):
            near = pl.ds(start + (pad + front - j), tile)
            picked = jnp.where(seg_pad[near, :] == own, conv_pad[near, :], 0.0)
            total = total + weight_ref[j : j + 1, :] * picked
            product = (glu * picked).reshape(tile // 8, 8, width)
            tap_acc[j] = tap_acc[j] + jnp.sum(product, axis=0)
        total = jnp.where(active_ref[part, :] > 0, total, 0.0)
        gate_sigmoid = jax.nn.sigmoid(gate_ref[part, :])
        dlin = total * gate_sigmoid
        dlin_ref[part, :] = dlin.astype(jnp.bfloat16)
        dgate_ref[part, :] = (dlin * linear_ref[part, :] * (1.0 - gate_sigmoid)).astype(
            jnp.bfloat16
        )

    tap_ref[...] = jnp.sum(tap_acc[...], axis=1)


def conv_both(projected, delta_swish, segment, active, weight, scale, shift):
    _, rows, given = projected.shape
    taps = weight.shape[0]
    width = 128
    channels = cdiv(given, width) * width

    def widen(array):
        extra = channels - given
        return jnp.pad(array, [(0, 0)] * (array.ndim - 1) + [(0, extra)]) if extra else array

    projected, delta_swish, weight = widen(projected), widen(delta_swish), widen(weight)
    scale, shift = widen(scale), widen(shift)
    tile = min(64, rows)
    padded = rows + 2 * taps
    column = pl.BlockSpec((rows, width), lambda c: (0, c))
    half = lambda h: pl.BlockSpec((None, rows, width), lambda c: (h, 0, c))
    row = pl.BlockSpec((1, width), lambda c: (0, c))
    whole = pl.BlockSpec((rows, 1), lambda c: (0, 0))
    results = pl.pallas_call(
        functools.partial(conv_kernel, taps, taps // 2, tile),
        grid=(channels // width,),
        out_shape=(
            jax.ShapeDtypeStruct((rows, channels), jnp.bfloat16),
            jax.ShapeDtypeStruct((rows, channels), jnp.bfloat16),
            jax.ShapeDtypeStruct((rows, channels), jnp.bfloat16),
            jax.ShapeDtypeStruct((taps, channels), jnp.float32),
        ),
        in_specs=[
            half(0),
            half(1),
            column,
            whole,
            whole,
            pl.BlockSpec((taps, width), lambda c: (0, c)),
            row,
            row,
        ],
        out_specs=[column, column, column, pl.BlockSpec((taps, width), lambda c: (0, c))],
        scratch_shapes=[
            pltpu.VMEM((padded, width), jnp.float32),
            pltpu.VMEM((padded, width), jnp.float32),
            pltpu.VMEM((padded, width), jnp.int32),
            pltpu.VMEM((taps, 8, width), jnp.float32),
        ],
        compiler_params=pltpu.CompilerParams(vmem_limit_bytes=24 * 1024 * 1024),
        cost_estimate=pl.CostEstimate(
            flops=10 * rows * channels * taps,
            bytes_accessed=18 * rows * channels,
            transcendentals=3 * rows * channels,
        ),
    )(
        projected,
        projected,
        delta_swish,
        segment[:, None],
        active.astype(jnp.int32)[:, None],
        weight,
        scale[None, :],
        shift[None, :],
    )
    return [result[:, :given] for result in results] if channels != given else results


def sum_kernel(chunk, per_array, orders, n, *refs):
    arrays = len(per_array)
    bits = len(orders[0])
    ins, small_in = refs[:arrays], refs[arrays]
    stacked_out, last_out, small_out = refs[arrays + 1 : arrays + 4]
    red, got, small_buf, small_got, sends, recvs, small_sends, small_recvs = refs[arrays + 4 :]
    me = lax.axis_index("dp")
    digit = [(me // (1 << b)) % 2 for b in range(bits)]
    partner = [me + (1 - 2 * digit[b]) * (1 << b) for b in range(bits)]
    places = [(a, i * chunk) for a in range(arrays) for i in range(per_array[a])]
    chunks = range(len(places))
    lengths = [chunk >> (s + 1) for s in range(bits)]
    bases = [chunk - 2 * lengths[s] for s in range(bits)]

    def target(c, start, size):
        a, first = places[c]
        rows = pl.ds(pl.multiple_of(first + start, 16), size)
        return stacked_out.at[a, rows] if a < arrays - 1 else last_out.at[rows]

    def held(c, s, start, size):
        if s == 0:
            a, first = places[c]
            return ins[a].at[pl.ds(pl.multiple_of(first + start, 16), size)]
        return red.at[c, pl.ds(pl.multiple_of(bases[s - 1] + start, 16), size)]

    def halving(c, s):
        b = orders[c][s]
        return pltpu.make_async_remote_copy(
            src_ref=held(c, s, (1 - digit[b]) * lengths[s], lengths[s]),
            dst_ref=got.at[c, pl.ds(bases[s], lengths[s])],
            send_sem=sends.at[s, c],
            recv_sem=recvs.at[s, c],
            device_id={"dp": partner[b]},
            device_id_type=pl.DeviceIdType.MESH,
        )

    def offset(c, s):
        return sum(digit[orders[c][k]] * lengths[k] for k in range(s + 1))

    def doubling(c, s):
        b = orders[c][s]
        place = target(c, offset(c, s), lengths[s])
        return pltpu.make_async_remote_copy(
            src_ref=place,
            dst_ref=place,
            send_sem=sends.at[bits + s, c],
            recv_sem=recvs.at[bits + s, c],
            device_id={"dp": partner[b]},
            device_id_type=pl.DeviceIdType.MESH,
        )

    def small_copy(s):
        return pltpu.make_async_remote_copy(
            src_ref=small_buf.at[s],
            dst_ref=small_got.at[s],
            send_sem=small_sends.at[s],
            recv_sem=small_recvs.at[s],
            device_id={"dp": partner[s]},
            device_id_type=pl.DeviceIdType.MESH,
        )

    barrier = pltpu.get_barrier_semaphore()
    for b in range(bits):
        pl.semaphore_signal(
            barrier, inc=1, device_id={"dp": partner[b]}, device_id_type=pl.DeviceIdType.MESH
        )
    pl.semaphore_wait(barrier, bits)

    small_buf[0] = small_in[...]
    small_copy(0).start()
    for c in chunks:
        halving(c, 0).start()
    for s in range(bits):
        for c in chunks:
            halving(c, s).wait_recv()
            kept = held(c, s, digit[orders[c][s]] * lengths[s], lengths[s])
            come = got.at[c, pl.ds(bases[s], lengths[s])]
            if s < bits - 1:
                into = red.at[c, pl.ds(bases[s], lengths[s])]
            else:
                into = target(c, offset(c, s), lengths[s])

            @pl.loop(0, lengths[s] // 16)
            def _(i):
                rows = pl.ds(pl.multiple_of(i * 16, 16), 16)
                into[rows, :] = (
                    kept[rows, :].astype(jnp.float32) + come[rows, :].astype(jnp.float32)
                ).astype(jnp.bfloat16)

            if s < bits - 1:
                halving(c, s + 1).start()
            else:
                doubling(c, s).start()
        small_copy(s).wait_recv()
        total = small_buf[s] + small_got[s]
        if s < bits - 1:
            small_buf[s + 1] = total
            small_copy(s + 1).start()
        else:
            small_out[...] = total
    for s in reversed(range(bits)):
        for c in chunks:
            doubling(c, s).wait_recv()
            if s > 0:
                doubling(c, s - 1).start()
    for s in range(bits):
        small_copy(s).wait_send()
        for c in chunks:
            halving(c, s).wait_send()
            doubling(c, s).wait_send()


def sum_over_dp(terms, small, n):
    rows, width = terms[0].shape
    bits = n.bit_length() - 1
    chunk = 16 * n
    per_array = [term.shape[0] // chunk for term in terms]
    count = sum(per_array)
    plain = list(range(bits))
    turned = [0] + plain[2:] + [1]
    orders = [turned if c % 4 == 0 and c < 8 else plain for c in range(count)]
    vmem = pl.BlockSpec(memory_space=pltpu.VMEM)
    return pl.pallas_call(
        functools.partial(sum_kernel, chunk, per_array, orders, n),
        out_shape=(
            jax.ShapeDtypeStruct((len(terms) - 1, rows, width), jnp.bfloat16),
            jax.ShapeDtypeStruct((rows, width), jnp.bfloat16),
            jax.ShapeDtypeStruct(small.shape, jnp.float32),
        ),
        in_specs=[vmem] * (len(terms) + 1),
        out_specs=(vmem, vmem, vmem),
        scratch_shapes=[
            pltpu.VMEM((count, chunk, width), jnp.bfloat16),
            pltpu.VMEM((count, chunk, width), jnp.bfloat16),
            pltpu.VMEM((bits,) + small.shape, jnp.float32),
            pltpu.VMEM((bits,) + small.shape, jnp.float32),
            pltpu.SemaphoreType.DMA((2 * bits, count)),
            pltpu.SemaphoreType.DMA((2 * bits, count)),
            pltpu.SemaphoreType.DMA((bits,)),
            pltpu.SemaphoreType.DMA((bits,)),
        ],
        compiler_params=pltpu.CompilerParams(
            collective_id=0, has_side_effects=True, vmem_limit_bytes=44 * 1024 * 1024
        ),
        cost_estimate=pl.CostEstimate(
            flops=count * chunk * width,
            bytes_accessed=4 * count * chunk * width,
            transcendentals=0,
        ),
    )(*terms, small)


def on_device(
    frames,
    norm_gain,
    norm_bias,
    input_weight,
    depth_weight,
    batch_scale,
    batch_shift,
    output_weight,
    upstream,
    replica_blocks,
    segment,
):
    replicas = lax.axis_size("dp")
    my_index = lax.axis_index("dp")
    tensor_index = lax.axis_index("tensor")
    full_width = norm_gain.shape[0]
    load_rows, part_width = frames.shape
    row_count = segment.shape[0]
    rows_part = upstream.shape[0]
    load_blocks = load_rows // BLK
    cap_blocks = row_count // BLK
    per_peer = cdiv(cap_blocks, replicas)
    row_start = tensor_index * rows_part
    column_start = tensor_index * part_width

    run_ends = jnp.cumsum(replica_blocks)
    starts = run_ends - replica_blocks
    peers = jnp.arange(replicas, dtype=jnp.int32)
    is_mine = peers == my_index
    my_start = jnp.sum(jnp.where(is_mine, starts, 0))
    my_blocks = jnp.sum(jnp.where(is_mine, replica_blocks, 0))
    my_end = my_start + my_blocks
    bucket = jnp.arange(per_peer, dtype=jnp.int32)
    first_out = cdiv(jnp.maximum(starts - my_index, 0), replicas)
    send_block = jnp.minimum(first_out[:, None] + bucket[None, :], load_blocks - 1)
    skipped = cdiv(jnp.maximum(my_start - peers, 0), replicas)
    arriving = peers[:, None] + replicas * (skipped[:, None] + bucket[None, :])
    landing = jnp.clip(arriving - my_start, 0, cap_blocks - 1)
    slots = jnp.arange(cap_blocks, dtype=jnp.int32)
    slot_number = my_start + slots
    slot_source = slot_number % replicas
    slot_skipped = cdiv(jnp.maximum(my_start - slot_source, 0), replicas)
    slot_pos = jnp.clip(slot_number // replicas - slot_skipped, 0, per_peer - 1)
    pick_in = slot_source * per_peer + slot_pos
    load_numbers = my_index + replicas * jnp.arange(load_blocks, dtype=jnp.int32)
    target = jnp.sum((run_ends[None, :] <= load_numbers[:, None]).astype(jnp.int32), axis=1)
    target_start = jnp.sum(jnp.where(peers[None, :] == target[:, None], starts[None, :], 0), axis=1)
    slot_out = jnp.arange(load_blocks, dtype=jnp.int32) - cdiv(
        jnp.maximum(target_start - my_index, 0), replicas
    )
    pick_back = target * per_peer + slot_out

    active = slots < my_blocks
    active_rows = jnp.repeat(active, BLK)
    active_mine = lax.dynamic_slice_in_dim(active_rows, row_start, rows_part)[:, None]

    delta_piece = jnp.where(active_mine, upstream, jnp.zeros_like(upstream))
    delta_whole = lax.all_gather(delta_piece, "tensor", axis=0, tiled=True)

    outbox = frames.reshape(load_blocks, BLK, part_width)[send_block.reshape(-1)]
    arrived = lax.all_to_all(
        outbox.reshape(replicas, per_peer, BLK, part_width),
        "dp",
        split_axis=0,
        concat_axis=0,
        tiled=True,
    )
    packed = jnp.where(
        active[:, None, None],
        arrived.reshape(replicas * per_peer, BLK, part_width)[pick_in],
        jnp.zeros((), jnp.bfloat16),
    )
    local_rows = packed.reshape(row_count, part_width)
    gathered = lax.all_gather(local_rows, "tensor", axis=1, tiled=True)

    delta_swish = lax.dot_general(
        delta_whole, output_weight, (((1,), (1,)), ((), ())), preferred_element_type=jnp.float32
    )

    gathered_float = gathered.astype(jnp.float32)
    center = jnp.mean(gathered_float, axis=1, keepdims=True)
    spread = jnp.mean(jnp.square(gathered_float - center), axis=1, keepdims=True)
    scale_row = lax.rsqrt(spread + epsilon)
    standard_full = (gathered_float - center) * scale_row
    normed = (standard_full * norm_gain + norm_bias).astype(jnp.bfloat16)
    projected = jnp.einsum("td,kcd->ktc", normed, input_weight, preferred_element_type=jnp.float32)

    swish, delta_linear, delta_gate, tap_local = conv_both(
        projected, delta_swish, segment, active_rows, depth_weight, batch_scale, batch_shift
    )

    back_term = (
        jnp.dot(delta_linear, input_weight[0], preferred_element_type=jnp.float32)
        + jnp.dot(delta_gate, input_weight[1], preferred_element_type=jnp.float32)
    ).astype(jnp.bfloat16)
    back_term, swish, delta_linear, delta_gate = lax.optimization_barrier(
        (back_term, swish, delta_linear, delta_gate)
    )
    delta_normed = lax.psum_scatter(back_term, "tensor", scatter_dimension=1, tiled=True).astype(
        jnp.float32
    )
    back_float = back_term.astype(jnp.float32)
    back_standard = back_float * standard_full
    unit_local = jnp.sum(back_float * norm_gain, axis=1)
    cross_local = jnp.sum(back_standard * norm_gain, axis=1)
    unit_total, cross_total = lax.psum((unit_local, cross_local), "tensor")
    norm_local = jnp.stack([jnp.sum(back_standard, axis=0), jnp.sum(back_float, axis=0)])

    mixed_sum = lax.psum_scatter(
        jnp.dot(swish, output_weight, preferred_element_type=jnp.float32).astype(jnp.bfloat16),
        "tensor",
        scatter_dimension=0,
        tiled=True,
    ).astype(jnp.float32)
    residual_part = lax.dynamic_slice_in_dim(gathered, row_start, rows_part, 0)
    block_output = jnp.where(
        active_mine, residual_part.astype(jnp.float32) + mixed_sum, 0.0
    ).astype(jnp.bfloat16)

    def over_rows(left, right):
        return lax.dot_general(
            left, right, (((0,), (0,)), ((), ())), preferred_element_type=jnp.float32
        ).astype(jnp.bfloat16)

    terms = (
        over_rows(delta_linear, normed),
        over_rows(delta_gate, normed),
        over_rows(swish, delta_whole),
    )

    gain_part = lax.dynamic_slice_in_dim(norm_gain, column_start, part_width)
    standard = (local_rows.astype(jnp.float32) - center) * scale_row
    delta_part = lax.dynamic_slice_in_dim(delta_whole, column_start, part_width, 1)
    delta_rows = delta_part.astype(jnp.float32) + scale_row * (
        delta_normed * gain_part
        - (unit_total / full_width)[:, None]
        - standard * (cross_total / full_width)[:, None]
    )
    delta_blocks = delta_rows.astype(jnp.bfloat16).reshape(cap_blocks, BLK, part_width)
    homebound = delta_blocks[landing.reshape(-1)].reshape(replicas, per_peer, BLK, part_width)

    taps = depth_weight.shape[0]
    small = jnp.concatenate([tap_local, norm_local.reshape(-1, part_width)])
    homebound, terms, small = lax.optimization_barrier((homebound, terms, small))
    if part_width % (16 * replicas) == 0 and replicas & (replicas - 1) == 0 and replicas > 2:
        weight_summed, out_summed, small_summed = sum_over_dp(terms, small, replicas)
    else:
        linear_summed, gate_summed, out_summed, small_summed = lax.psum((*terms, small), "dp")
        weight_summed = jnp.stack([linear_summed, gate_summed])
    tap_summed = small_summed[:taps]
    norm_part = lax.psum_scatter(
        small_summed[taps:].reshape(2, full_width), "tensor", scatter_dimension=1, tiled=True
    )
    returned = lax.all_to_all(homebound, "dp", split_axis=0, concat_axis=0, tiled=True)
    frame_gradient = returned.reshape(replicas * per_peer, BLK, part_width)[pick_back].reshape(
        load_rows, part_width
    )
    return (
        block_output,
        frame_gradient,
        weight_summed,
        out_summed,
        tap_summed,
        norm_part[0],
        norm_part[1],
    )


def solution(mesh):
    in_specs = (
        P("dp", "tensor"),
        P(),
        P(),
        P(None, "tensor", None),
        P(None, "tensor"),
        P("tensor"),
        P("tensor"),
        P("tensor", None),
        P(("dp", "tensor"), None),
        P(),
        P("dp"),
    )
    out_specs = (
        P(("dp", "tensor"), None),
        P("dp", "tensor"),
        P(None, "tensor", None),
        P("tensor", None),
        P(None, "tensor"),
        P("tensor"),
        P("tensor"),
    )
    return jax.shard_map(
        on_device, mesh=mesh, in_specs=in_specs, out_specs=out_specs, check_vma=False
    )
```

```python
import functools

import jax
import jax.numpy as jnp
from jax import lax
from jax.experimental import pallas as pl
from jax.experimental.pallas import tpu as pltpu
from jax.sharding import PartitionSpec as P

BLK = 8


epsilon = 1e-05


def cdiv(a, b):
    return (a + b - 1) // b


def conv_kernel(
    taps,
    front,
    tile,
    linear_ref,
    gate_ref,
    delta_ref,
    seg_ref,
    active_ref,
    weight_ref,
    scale_ref,
    shift_ref,
    swish_ref,
    dlin_ref,
    dgate_ref,
    tap_ref,
    glu_pad,
    conv_pad,
    seg_pad,
    tap_acc,
):
    rows, width = linear_ref.shape
    pad = taps
    padded = rows + 2 * pad

    zeros = jnp.zeros((pad, width), jnp.float32)
    glu_pad[0:pad, :] = zeros
    glu_pad[pad + rows : padded, :] = zeros
    conv_pad[0:pad, :] = zeros
    conv_pad[pad + rows : padded, :] = zeros

    @pl.when(pl.program_id(0) == 0)
    def _():
        outside = jnp.full((pad, width), -1, jnp.int32)
        seg_pad[0:pad, :] = outside
        seg_pad[pad + rows : padded, :] = outside
        seg_pad[pad : pad + rows, :] = jnp.broadcast_to(seg_ref[...], (rows, width))

    tap_acc[...] = jnp.zeros_like(tap_acc)

    for start in range(0, rows, tile):
        part = pl.ds(start, tile)
        glu = linear_ref[part, :] * jax.nn.sigmoid(gate_ref[part, :])
        glu = glu.astype(jnp.bfloat16).astype(jnp.float32)
        glu_pad[pl.ds(pad + start, tile), :] = jnp.where(active_ref[part, :] > 0, glu, 0.0)

    @pl.loop(0, rows // tile)
    def _(step):
        start = pl.multiple_of(step * tile, tile)
        part = pl.ds(start, tile)
        own = seg_pad[pl.ds(pad + start, tile), :]
        total = jnp.zeros((tile, width), jnp.float32)
        for j in range(taps):
            near = pl.ds(start + (pad + j - front), tile)
            picked = jnp.where(seg_pad[near, :] == own, glu_pad[near, :], 0.0)
            total = total + weight_ref[j : j + 1, :] * picked
        scale = scale_ref[...]
        preswish = total * scale + shift_ref[...]
        pre_sigmoid = jax.nn.sigmoid(preswish)
        swish_ref[part, :] = (preswish * pre_sigmoid).astype(jnp.bfloat16)
        conv_pad[pl.ds(pad + start, tile), :] = (
            delta_ref[part, :]
            * pre_sigmoid
            * (1.0 + preswish * (1.0 - pre_sigmoid))
            * scale
        )

    @pl.loop(0, rows // tile)
    def _(step):
        start = pl.multiple_of(step * tile, tile)
        part = pl.ds(start, tile)
        own = seg_pad[pl.ds(pad + start, tile), :]
        glu = glu_pad[pl.ds(pad + start, tile), :]
        total = jnp.zeros((tile, width), jnp.float32)
        for j in range(taps):
            near = pl.ds(start + (pad + front - j), tile)
            picked = jnp.where(seg_pad[near, :] == own, conv_pad[near, :], 0.0)
            total = total + weight_ref[j : j + 1, :] * picked
            product = (glu * picked).reshape(tile // 8, 8, width)
            tap_acc[j] = tap_acc[j] + jnp.sum(product, axis=0)
        total = jnp.where(active_ref[part, :] > 0, total, 0.0)
        gate_sigmoid = jax.nn.sigmoid(gate_ref[part, :])
        dlin = total * gate_sigmoid
        dlin_ref[part, :] = dlin.astype(jnp.bfloat16)
        dgate_ref[part, :] = (dlin * linear_ref[part, :] * (1.0 - gate_sigmoid)).astype(
            jnp.bfloat16
        )

    tap_ref[...] = jnp.sum(tap_acc[...], axis=1)


def conv_both(projected, delta_swish, segment, active, weight, scale, shift):
    _, rows, given = projected.shape
    taps = weight.shape[0]
    width = 128
    channels = cdiv(given, width) * width

    def widen(array):
        extra = channels - given
        return jnp.pad(array, [(0, 0)] * (array.ndim - 1) + [(0, extra)]) if extra else array

    projected, delta_swish, weight = widen(projected), widen(delta_swish), widen(weight)
    scale, shift = widen(scale), widen(shift)
    tile = min(64, rows)
    padded = rows + 2 * taps
    column = pl.BlockSpec((rows, width), lambda c: (0, c))
    half = lambda h: pl.BlockSpec((None, rows, width), lambda c: (h, 0, c))
    row = pl.BlockSpec((1, width), lambda c: (0, c))
    whole = pl.BlockSpec((rows, 1), lambda c: (0, 0))
    results = pl.pallas_call(
        functools.partial(conv_kernel, taps, taps // 2, tile),
        grid=(channels // width,),
        out_shape=(
            jax.ShapeDtypeStruct((rows, channels), jnp.bfloat16),
            jax.ShapeDtypeStruct((rows, channels), jnp.bfloat16),
            jax.ShapeDtypeStruct((rows, channels), jnp.bfloat16),
            jax.ShapeDtypeStruct((taps, channels), jnp.float32),
        ),
        in_specs=[
            half(0),
            half(1),
            column,
            whole,
            whole,
            pl.BlockSpec((taps, width), lambda c: (0, c)),
            row,
            row,
        ],
        out_specs=[column, column, column, pl.BlockSpec((taps, width), lambda c: (0, c))],
        scratch_shapes=[
            pltpu.VMEM((padded, width), jnp.float32),
            pltpu.VMEM((padded, width), jnp.float32),
            pltpu.VMEM((padded, width), jnp.int32),
            pltpu.VMEM((taps, 8, width), jnp.float32),
        ],
        compiler_params=pltpu.CompilerParams(vmem_limit_bytes=24 * 1024 * 1024),
        cost_estimate=pl.CostEstimate(
            flops=10 * rows * channels * taps,
            bytes_accessed=18 * rows * channels,
            transcendentals=3 * rows * channels,
        ),
    )(
        projected,
        projected,
        delta_swish,
        segment[:, None],
        active.astype(jnp.int32)[:, None],
        weight,
        scale[None, :],
        shift[None, :],
    )
    return [result[:, :given] for result in results] if channels != given else results


def sum_kernel(chunk, per_array, orders, with_small, *refs):
    arrays = len(per_array)
    bits = len(orders[0])
    ins, refs = refs[:arrays], refs[arrays:]
    if with_small:
        small_in, stacked_out, small_out, red, got, sends, recvs = refs[:7]
        small_buf, small_got, small_sends, small_recvs = refs[7:]
    else:
        stacked_out, red, got, sends, recvs = refs
    me = lax.axis_index("dp")
    digit = [(me // (1 << b)) % 2 for b in range(bits)]
    partner = [me + (1 - 2 * digit[b]) * (1 << b) for b in range(bits)]
    places = [(a, i * chunk) for a in range(arrays) for i in range(per_array[a])]
    chunks = range(len(places))
    lengths = [chunk >> (s + 1) for s in range(bits)]
    bases = [chunk - 2 * lengths[s] for s in range(bits)]

    def target(c, start, size):
        a, first = places[c]
        rows = pl.ds(pl.multiple_of(first + start, 16), size)
        return stacked_out.at[a, rows]

    def held(c, s, start, size):
        if s == 0:
            a, first = places[c]
            return ins[a].at[pl.ds(pl.multiple_of(first + start, 16), size)]
        return red.at[c, pl.ds(pl.multiple_of(bases[s - 1] + start, 16), size)]

    def halving(c, s):
        b = orders[c][s]
        return pltpu.make_async_remote_copy(
            src_ref=held(c, s, (1 - digit[b]) * lengths[s], lengths[s]),
            dst_ref=got.at[c, pl.ds(bases[s], lengths[s])],
            send_sem=sends.at[s, c],
            recv_sem=recvs.at[s, c],
            device_id={"dp": partner[b]},
            device_id_type=pl.DeviceIdType.MESH,
        )

    def offset(c, s):
        return sum(digit[orders[c][k]] * lengths[k] for k in range(s + 1))

    def doubling(c, s):
        b = orders[c][s]
        place = target(c, offset(c, s), lengths[s])
        return pltpu.make_async_remote_copy(
            src_ref=place,
            dst_ref=place,
            send_sem=sends.at[bits + s, c],
            recv_sem=recvs.at[bits + s, c],
            device_id={"dp": partner[b]},
            device_id_type=pl.DeviceIdType.MESH,
        )

    def small_copy(s):
        return pltpu.make_async_remote_copy(
            src_ref=small_buf.at[s],
            dst_ref=small_got.at[s],
            send_sem=small_sends.at[s],
            recv_sem=small_recvs.at[s],
            device_id={"dp": partner[s]},
            device_id_type=pl.DeviceIdType.MESH,
        )

    barrier = pltpu.get_barrier_semaphore()
    for b in range(bits):
        pl.semaphore_signal(
            barrier, inc=1, device_id={"dp": partner[b]}, device_id_type=pl.DeviceIdType.MESH
        )
    pl.semaphore_wait(barrier, bits)

    if with_small:
        small_buf[0] = small_in[...]
        small_copy(0).start()
    for c in chunks:
        halving(c, 0).start()
    for s in range(bits):
        for c in chunks:
            halving(c, s).wait_recv()
            kept = held(c, s, digit[orders[c][s]] * lengths[s], lengths[s])
            come = got.at[c, pl.ds(bases[s], lengths[s])]
            if s < bits - 1:
                into = red.at[c, pl.ds(bases[s], lengths[s])]
            else:
                into = target(c, offset(c, s), lengths[s])

            @pl.loop(0, lengths[s] // 16)
            def _(i):
                rows = pl.ds(pl.multiple_of(i * 16, 16), 16)
                into[rows, :] = (
                    kept[rows, :].astype(jnp.float32) + come[rows, :].astype(jnp.float32)
                ).astype(jnp.bfloat16)

            if s < bits - 1:
                halving(c, s + 1).start()
            else:
                doubling(c, s).start()
        if with_small:
            small_copy(s).wait_recv()
            total = small_buf[s] + small_got[s]
            if s < bits - 1:
                small_buf[s + 1] = total
                small_copy(s + 1).start()
            else:
                small_out[...] = total
    for s in reversed(range(bits)):
        for c in chunks:
            doubling(c, s).wait_recv()
            if s > 0:
                doubling(c, s - 1).start()
    for s in range(bits):
        if with_small:
            small_copy(s).wait_send()
        for c in chunks:
            halving(c, s).wait_send()
            doubling(c, s).wait_send()


def sum_over_dp(terms, n, collective_id, small=None):
    rows, width = terms[0].shape
    bits = n.bit_length() - 1
    chunk = 16 * n
    per_array = [rows // chunk] * len(terms)
    count = sum(per_array)
    plain = list(range(bits))
    turned = [0] + plain[2:] + [1]
    orders = [turned if c % 4 == 0 and c + 2 < count else plain for c in range(count)]
    vmem = pl.BlockSpec(memory_space=pltpu.VMEM)
    with_small = small is not None
    extra = (small,) if with_small else ()
    small_shapes = [pltpu.VMEM((bits,) + e.shape, jnp.float32) for e in extra * 2]
    small_semaphores = [pltpu.SemaphoreType.DMA((bits,)) for e in extra * 2]
    return pl.pallas_call(
        functools.partial(sum_kernel, chunk, per_array, orders, with_small),
        out_shape=[jax.ShapeDtypeStruct((len(terms), rows, width), jnp.bfloat16)]
        + [jax.ShapeDtypeStruct(e.shape, jnp.float32) for e in extra],
        in_specs=[vmem] * (len(terms) + len(extra)),
        out_specs=[vmem] * (1 + len(extra)),
        scratch_shapes=[
            pltpu.VMEM((count, chunk, width), jnp.bfloat16),
            pltpu.VMEM((count, chunk, width), jnp.bfloat16),
            pltpu.SemaphoreType.DMA((2 * bits, count)),
            pltpu.SemaphoreType.DMA((2 * bits, count)),
        ]
        + small_shapes
        + small_semaphores,
        compiler_params=pltpu.CompilerParams(
            collective_id=collective_id, has_side_effects=True, vmem_limit_bytes=36 * 1024 * 1024
        ),
        cost_estimate=pl.CostEstimate(
            flops=count * chunk * width,
            bytes_accessed=4 * count * chunk * width,
            transcendentals=0,
        ),
    )(*terms, *extra)


def on_device(
    frames,
    norm_gain,
    norm_bias,
    input_weight,
    depth_weight,
    batch_scale,
    batch_shift,
    output_weight,
    upstream,
    replica_blocks,
    segment,
):
    replicas = lax.axis_size("dp")
    my_index = lax.axis_index("dp")
    tensor_index = lax.axis_index("tensor")
    full_width = norm_gain.shape[0]
    load_rows, part_width = frames.shape
    row_count = segment.shape[0]
    rows_part = upstream.shape[0]
    load_blocks = load_rows // BLK
    cap_blocks = row_count // BLK
    per_peer = cdiv(cap_blocks, replicas)
    row_start = tensor_index * rows_part
    column_start = tensor_index * part_width

    run_ends = jnp.cumsum(replica_blocks)
    starts = run_ends - replica_blocks
    peers = jnp.arange(replicas, dtype=jnp.int32)
    is_mine = peers == my_index
    my_start = jnp.sum(jnp.where(is_mine, starts, 0))
    my_blocks = jnp.sum(jnp.where(is_mine, replica_blocks, 0))
    my_end = my_start + my_blocks
    bucket = jnp.arange(per_peer, dtype=jnp.int32)
    first_out = cdiv(jnp.maximum(starts - my_index, 0), replicas)
    send_block = jnp.minimum(first_out[:, None] + bucket[None, :], load_blocks - 1)
    skipped = cdiv(jnp.maximum(my_start - peers, 0), replicas)
    arriving = peers[:, None] + replicas * (skipped[:, None] + bucket[None, :])
    landing = jnp.clip(arriving - my_start, 0, cap_blocks - 1)
    slots = jnp.arange(cap_blocks, dtype=jnp.int32)
    slot_number = my_start + slots
    slot_source = slot_number % replicas
    slot_skipped = cdiv(jnp.maximum(my_start - slot_source, 0), replicas)
    slot_pos = jnp.clip(slot_number // replicas - slot_skipped, 0, per_peer - 1)
    pick_in = slot_source * per_peer + slot_pos
    load_numbers = my_index + replicas * jnp.arange(load_blocks, dtype=jnp.int32)
    target = jnp.sum((run_ends[None, :] <= load_numbers[:, None]).astype(jnp.int32), axis=1)
    target_start = jnp.sum(jnp.where(peers[None, :] == target[:, None], starts[None, :], 0), axis=1)
    slot_out = jnp.arange(load_blocks, dtype=jnp.int32) - cdiv(
        jnp.maximum(target_start - my_index, 0), replicas
    )
    pick_back = target * per_peer + slot_out

    active = slots < my_blocks
    active_rows = jnp.repeat(active, BLK)
    active_mine = lax.dynamic_slice_in_dim(active_rows, row_start, rows_part)[:, None]

    upstream_whole = lax.all_gather(upstream, "tensor", axis=0, tiled=True)
    delta_whole = jnp.where(active_rows[:, None], upstream_whole, jnp.zeros_like(upstream_whole))

    outbox = frames.reshape(load_blocks, BLK, part_width)[send_block.reshape(-1)]
    arrived = lax.all_to_all(
        outbox.reshape(replicas, per_peer, BLK, part_width),
        "dp",
        split_axis=0,
        concat_axis=0,
        tiled=True,
    )
    packed = jnp.where(
        active[:, None, None],
        arrived.reshape(replicas * per_peer, BLK, part_width)[pick_in],
        jnp.zeros((), jnp.bfloat16),
    )
    local_rows = packed.reshape(row_count, part_width)
    gathered = lax.all_gather(local_rows, "tensor", axis=1, tiled=True)

    delta_swish = lax.dot_general(
        delta_whole, output_weight, (((1,), (1,)), ((), ())), preferred_element_type=jnp.float32
    )

    gathered_float = gathered.astype(jnp.float32)
    center = jnp.mean(gathered_float, axis=1, keepdims=True)
    spread = jnp.mean(jnp.square(gathered_float - center), axis=1, keepdims=True)
    scale_row = lax.rsqrt(spread + epsilon)
    standard_full = (gathered_float - center) * scale_row
    normed = (standard_full * norm_gain + norm_bias).astype(jnp.bfloat16)
    projected = jnp.einsum("td,kcd->ktc", normed, input_weight, preferred_element_type=jnp.float32)

    swish, delta_linear, delta_gate, tap_local = conv_both(
        projected, delta_swish, segment, active_rows, depth_weight, batch_scale, batch_shift
    )

    back_term = (
        jnp.dot(delta_linear, input_weight[0], preferred_element_type=jnp.float32)
        + jnp.dot(delta_gate, input_weight[1], preferred_element_type=jnp.float32)
    ).astype(jnp.bfloat16)
    back_term, swish, delta_linear, delta_gate = lax.optimization_barrier(
        (back_term, swish, delta_linear, delta_gate)
    )
    delta_normed = lax.psum_scatter(back_term, "tensor", scatter_dimension=1, tiled=True).astype(
        jnp.float32
    )
    mixed_term = jnp.dot(swish, output_weight, preferred_element_type=jnp.float32).astype(
        jnp.bfloat16
    )
    mixed_sum = lax.psum_scatter(
        mixed_term, "tensor", scatter_dimension=0, tiled=True
    ).astype(jnp.float32)
    back_float = back_term.astype(jnp.float32) * norm_gain
    unit_local = jnp.sum(back_float, axis=1)
    cross_local = jnp.sum(back_float * standard_full, axis=1)
    unit_total, cross_total = lax.psum((unit_local, cross_local), "tensor")

    def over_rows(left, right):
        return lax.dot_general(
            left, right, (((0,), (0,)), ((), ())), preferred_element_type=jnp.float32
        ).astype(jnp.bfloat16)

    by_kernel = (
        part_width % (16 * replicas) == 0 and replicas & (replicas - 1) == 0 and replicas > 2
    )
    terms = (over_rows(delta_linear, normed), over_rows(delta_gate, normed))
    if by_kernel:
        terms, mixed_term, swish = lax.optimization_barrier((terms, mixed_term, swish))
        weight_summed = sum_over_dp(terms, replicas, 1)[0]
        delta_normed, swish, weight_summed = lax.optimization_barrier(
            (delta_normed, swish, weight_summed)
        )
    else:
        weight_summed = lax.psum(jnp.stack(terms), "dp")
    out_term = over_rows(swish, delta_whole)

    residual_part = lax.dynamic_slice_in_dim(gathered, row_start, rows_part, 0)
    block_output = jnp.where(
        active_mine, residual_part.astype(jnp.float32) + mixed_sum, 0.0
    ).astype(jnp.bfloat16)

    gain_part = lax.dynamic_slice_in_dim(norm_gain, column_start, part_width)
    standard = (local_rows.astype(jnp.float32) - center) * scale_row
    delta_part = lax.dynamic_slice_in_dim(delta_whole, column_start, part_width, 1)
    delta_rows = delta_part.astype(jnp.float32) + scale_row * (
        delta_normed * gain_part
        - (unit_total / full_width)[:, None]
        - standard * (cross_total / full_width)[:, None]
    )
    delta_blocks = delta_rows.astype(jnp.bfloat16).reshape(cap_blocks, BLK, part_width)
    homebound = delta_blocks[landing.reshape(-1)].reshape(replicas, per_peer, BLK, part_width)

    taps = depth_weight.shape[0]
    norm_local = jnp.stack([jnp.sum(delta_normed * standard, axis=0), jnp.sum(delta_normed, axis=0)])
    small = jnp.concatenate([tap_local, norm_local])
    homebound, out_term, small = lax.optimization_barrier((homebound, out_term, small))
    if by_kernel:
        out_stack, small_summed = sum_over_dp((out_term,), replicas, 2, small)
        out_summed = out_stack[0]
    else:
        out_summed, small_summed = lax.psum((out_term, small), "dp")
    returned = lax.all_to_all(homebound, "dp", split_axis=0, concat_axis=0, tiled=True)
    frame_gradient = returned.reshape(replicas * per_peer, BLK, part_width)[pick_back].reshape(
        load_rows, part_width
    )
    return (
        block_output,
        frame_gradient,
        weight_summed,
        out_summed,
        small_summed[:taps],
        small_summed[taps],
        small_summed[taps + 1],
    )


def solution(mesh):
    in_specs = (
        P("dp", "tensor"),
        P(),
        P(),
        P(None, "tensor", None),
        P(None, "tensor"),
        P("tensor"),
        P("tensor"),
        P("tensor", None),
        P(("dp", "tensor"), None),
        P(),
        P("dp"),
    )
    out_specs = (
        P(("dp", "tensor"), None),
        P("dp", "tensor"),
        P(None, "tensor", None),
        P("tensor", None),
        P(None, "tensor"),
        P("tensor"),
        P("tensor"),
    )
    return jax.shard_map(
        on_device, mesh=mesh, in_specs=in_specs, out_specs=out_specs, check_vma=False
    )
```

```python
import functools

import jax
import jax.numpy as jnp
from jax import lax
from jax.experimental import pallas as pl
from jax.experimental.pallas import tpu as pltpu
from jax.sharding import PartitionSpec as P

BLK = 8


epsilon = 1e-05


def cdiv(a, b):
    return (a + b - 1) // b


def conv_kernel(
    taps,
    front,
    tile,
    linear_ref,
    gate_ref,
    delta_ref,
    seg_ref,
    active_ref,
    weight_ref,
    scale_ref,
    shift_ref,
    swish_ref,
    dlin_ref,
    dgate_ref,
    tap_ref,
    glu_pad,
    conv_pad,
    seg_pad,
    tap_acc,
):
    rows, width = linear_ref.shape
    pad = taps
    padded = rows + 2 * pad

    zeros = jnp.zeros((pad, width), jnp.float32)
    glu_pad[0:pad, :] = zeros
    glu_pad[pad + rows : padded, :] = zeros
    conv_pad[0:pad, :] = zeros
    conv_pad[pad + rows : padded, :] = zeros

    @pl.when(pl.program_id(0) == 0)
    def _():
        outside = jnp.full((pad, width), -1, jnp.int32)
        seg_pad[0:pad, :] = outside
        seg_pad[pad + rows : padded, :] = outside
        seg_pad[pad : pad + rows, :] = jnp.broadcast_to(seg_ref[...], (rows, width))

    tap_acc[...] = jnp.zeros_like(tap_acc)

    for start in range(0, rows, tile):
        part = pl.ds(start, tile)
        glu = linear_ref[part, :] * jax.nn.sigmoid(gate_ref[part, :])
        glu = glu.astype(jnp.bfloat16).astype(jnp.float32)
        glu_pad[pl.ds(pad + start, tile), :] = jnp.where(active_ref[part, :] > 0, glu, 0.0)

    @pl.loop(0, rows // tile)
    def _(step):
        start = pl.multiple_of(step * tile, tile)
        part = pl.ds(start, tile)
        own = seg_pad[pl.ds(pad + start, tile), :]
        total = jnp.zeros((tile, width), jnp.float32)
        for j in range(taps):
            near = pl.ds(start + (pad + j - front), tile)
            picked = jnp.where(seg_pad[near, :] == own, glu_pad[near, :], 0.0)
            total = total + weight_ref[j : j + 1, :] * picked
        scale = scale_ref[...]
        preswish = total * scale + shift_ref[...]
        pre_sigmoid = jax.nn.sigmoid(preswish)
        swish_ref[part, :] = (preswish * pre_sigmoid).astype(jnp.bfloat16)
        conv_pad[pl.ds(pad + start, tile), :] = (
            delta_ref[part, :]
            * pre_sigmoid
            * (1.0 + preswish * (1.0 - pre_sigmoid))
            * scale
        )

    @pl.loop(0, rows // tile)
    def _(step):
        start = pl.multiple_of(step * tile, tile)
        part = pl.ds(start, tile)
        own = seg_pad[pl.ds(pad + start, tile), :]
        glu = glu_pad[pl.ds(pad + start, tile), :]
        total = jnp.zeros((tile, width), jnp.float32)
        for j in range(taps):
            near = pl.ds(start + (pad + front - j), tile)
            picked = jnp.where(seg_pad[near, :] == own, conv_pad[near, :], 0.0)
            total = total + weight_ref[j : j + 1, :] * picked
            product = (glu * picked).reshape(tile // 8, 8, width)
            tap_acc[j] = tap_acc[j] + jnp.sum(product, axis=0)
        total = jnp.where(active_ref[part, :] > 0, total, 0.0)
        gate_sigmoid = jax.nn.sigmoid(gate_ref[part, :])
        dlin = total * gate_sigmoid
        dlin_ref[part, :] = dlin.astype(jnp.bfloat16)
        dgate_ref[part, :] = (dlin * linear_ref[part, :] * (1.0 - gate_sigmoid)).astype(
            jnp.bfloat16
        )

    tap_ref[...] = jnp.sum(tap_acc[...], axis=1)


def conv_both(projected, delta_swish, segment, active, weight, scale, shift):
    _, rows, given = projected.shape
    taps = weight.shape[0]
    width = 128
    channels = cdiv(given, width) * width

    def widen(array):
        extra = channels - given
        return jnp.pad(array, [(0, 0)] * (array.ndim - 1) + [(0, extra)]) if extra else array

    projected, delta_swish, weight = widen(projected), widen(delta_swish), widen(weight)
    scale, shift = widen(scale), widen(shift)
    tile = min(64, rows)
    padded = rows + 2 * taps
    column = pl.BlockSpec((rows, width), lambda c: (0, c))
    half = lambda h: pl.BlockSpec((None, rows, width), lambda c: (h, 0, c))
    row = pl.BlockSpec((1, width), lambda c: (0, c))
    whole = pl.BlockSpec((rows, 1), lambda c: (0, 0))
    results = pl.pallas_call(
        functools.partial(conv_kernel, taps, taps // 2, tile),
        grid=(channels // width,),
        out_shape=(
            jax.ShapeDtypeStruct((rows, channels), jnp.bfloat16),
            jax.ShapeDtypeStruct((rows, channels), jnp.bfloat16),
            jax.ShapeDtypeStruct((rows, channels), jnp.bfloat16),
            jax.ShapeDtypeStruct((taps, channels), jnp.float32),
        ),
        in_specs=[
            half(0),
            half(1),
            column,
            whole,
            whole,
            pl.BlockSpec((taps, width), lambda c: (0, c)),
            row,
            row,
        ],
        out_specs=[column, column, column, pl.BlockSpec((taps, width), lambda c: (0, c))],
        scratch_shapes=[
            pltpu.VMEM((padded, width), jnp.float32),
            pltpu.VMEM((padded, width), jnp.float32),
            pltpu.VMEM((padded, width), jnp.int32),
            pltpu.VMEM((taps, 8, width), jnp.float32),
        ],
        compiler_params=pltpu.CompilerParams(vmem_limit_bytes=24 * 1024 * 1024),
        cost_estimate=pl.CostEstimate(
            flops=10 * rows * channels * taps,
            bytes_accessed=18 * rows * channels,
            transcendentals=3 * rows * channels,
        ),
    )(
        projected,
        projected,
        delta_swish,
        segment[:, None],
        active.astype(jnp.int32)[:, None],
        weight,
        scale[None, :],
        shift[None, :],
    )
    return [result[:, :given] for result in results] if channels != given else results


def sum_kernel(chunk, per_array, orders, with_small, *refs):
    arrays = len(per_array)
    bits = len(orders[0])
    ins, refs = refs[:arrays], refs[arrays:]
    if with_small:
        small_in, stacked_out, small_out, red, got, sends, recvs = refs[:7]
        small_buf, small_got, small_sends, small_recvs = refs[7:]
    else:
        stacked_out, red, got, sends, recvs = refs
    me = lax.axis_index("dp")
    digit = [(me // (1 << b)) % 2 for b in range(bits)]
    partner = [me + (1 - 2 * digit[b]) * (1 << b) for b in range(bits)]
    places = [(a, i * chunk) for a in range(arrays) for i in range(per_array[a])]
    chunks = range(len(places))
    lengths = [chunk >> (s + 1) for s in range(bits)]
    bases = [chunk - 2 * lengths[s] for s in range(bits)]

    def target(c, start, size):
        a, first = places[c]
        rows = pl.ds(pl.multiple_of(first + start, 16), size)
        return stacked_out.at[a, rows]

    def held(c, s, start, size):
        if s == 0:
            a, first = places[c]
            return ins[a].at[pl.ds(pl.multiple_of(first + start, 16), size)]
        return red.at[c, pl.ds(pl.multiple_of(bases[s - 1] + start, 16), size)]

    def halving(c, s):
        b = orders[c][s]
        return pltpu.make_async_remote_copy(
            src_ref=held(c, s, (1 - digit[b]) * lengths[s], lengths[s]),
            dst_ref=got.at[c, pl.ds(bases[s], lengths[s])],
            send_sem=sends.at[s, c],
            recv_sem=recvs.at[s, c],
            device_id={"dp": partner[b]},
            device_id_type=pl.DeviceIdType.MESH,
        )

    def offset(c, s):
        return sum(digit[orders[c][k]] * lengths[k] for k in range(s + 1))

    def doubling(c, s):
        b = orders[c][s]
        place = target(c, offset(c, s), lengths[s])
        return pltpu.make_async_remote_copy(
            src_ref=place,
            dst_ref=place,
            send_sem=sends.at[bits + s, c],
            recv_sem=recvs.at[bits + s, c],
            device_id={"dp": partner[b]},
            device_id_type=pl.DeviceIdType.MESH,
        )

    def small_copy(s):
        return pltpu.make_async_remote_copy(
            src_ref=small_buf.at[s],
            dst_ref=small_got.at[s],
            send_sem=small_sends.at[s],
            recv_sem=small_recvs.at[s],
            device_id={"dp": partner[s]},
            device_id_type=pl.DeviceIdType.MESH,
        )

    barrier = pltpu.get_barrier_semaphore()
    for b in range(bits):
        pl.semaphore_signal(
            barrier, inc=1, device_id={"dp": partner[b]}, device_id_type=pl.DeviceIdType.MESH
        )
    pl.semaphore_wait(barrier, bits)

    if with_small:
        small_buf[0] = small_in[...]
        small_copy(0).start()
    for c in chunks:
        halving(c, 0).start()

    def halving_done(c, s):
        halving(c, s).wait_recv()
        kept = held(c, s, digit[orders[c][s]] * lengths[s], lengths[s])
        come = got.at[c, pl.ds(bases[s], lengths[s])]
        if s < bits - 1:
            into = red.at[c, pl.ds(bases[s], lengths[s])]
        else:
            into = target(c, offset(c, s), lengths[s])

        @pl.loop(0, lengths[s] // 16)
        def _(i):
            rows = pl.ds(pl.multiple_of(i * 16, 16), 16)
            into[rows, :] = (
                kept[rows, :].astype(jnp.float32) + come[rows, :].astype(jnp.float32)
            ).astype(jnp.bfloat16)

        if s < bits - 1:
            halving(c, s + 1).start()
        else:
            doubling(c, s).start()

    def doubling_done(c, s):
        doubling(c, s).wait_recv()
        if s > 0:
            doubling(c, s - 1).start()

    def small_done(s):
        small_copy(s).wait_recv()
        total = small_buf[s] + small_got[s]
        if s < bits - 1:
            small_buf[s + 1] = total
            small_copy(s + 1).start()
        else:
            small_out[...] = total

    events = [(c + 2 * k, k, c) for c in chunks for k in range(2 * bits)]
    for _, k, c in sorted(events):
        if k < bits:
            halving_done(c, k)
            if with_small and c == 0:
                small_done(k)
        else:
            doubling_done(c, 2 * bits - 1 - k)
    for s in range(bits):
        if with_small:
            small_copy(s).wait_send()
        for c in chunks:
            halving(c, s).wait_send()
            doubling(c, s).wait_send()


def sum_over_dp(terms, n, collective_id, small=None):
    rows, width = terms[0].shape
    bits = n.bit_length() - 1
    chunk = 16 * n
    per_array = [rows // chunk] * len(terms)
    count = sum(per_array)
    plain = list(range(bits))
    turned = [0] + plain[2:] + [1]
    orders = [turned if c == 0 else plain for c in range(count)]
    vmem = pl.BlockSpec(memory_space=pltpu.VMEM)
    with_small = small is not None
    extra = (small,) if with_small else ()
    small_shapes = [pltpu.VMEM((bits,) + e.shape, jnp.float32) for e in extra * 2]
    small_semaphores = [pltpu.SemaphoreType.DMA((bits,)) for e in extra * 2]
    return pl.pallas_call(
        functools.partial(sum_kernel, chunk, per_array, orders, with_small),
        out_shape=[jax.ShapeDtypeStruct((len(terms), rows, width), jnp.bfloat16)]
        + [jax.ShapeDtypeStruct(e.shape, jnp.float32) for e in extra],
        in_specs=[vmem] * (len(terms) + len(extra)),
        out_specs=[vmem] * (1 + len(extra)),
        scratch_shapes=[
            pltpu.VMEM((count, chunk, width), jnp.bfloat16),
            pltpu.VMEM((count, chunk, width), jnp.bfloat16),
            pltpu.SemaphoreType.DMA((2 * bits, count)),
            pltpu.SemaphoreType.DMA((2 * bits, count)),
        ]
        + small_shapes
        + small_semaphores,
        compiler_params=pltpu.CompilerParams(
            collective_id=collective_id, has_side_effects=True, vmem_limit_bytes=44 * 1024 * 1024
        ),
        cost_estimate=pl.CostEstimate(
            flops=count * chunk * width,
            bytes_accessed=4 * count * chunk * width,
            transcendentals=0,
        ),
    )(*terms, *extra)


def exchange_kernel(mine_ref, full_ref, own_sem, send_sem, recv_sem):
    width = mine_ref.shape[1]
    me = lax.axis_index("tensor")
    other = {"tensor": 1 - me}
    columns = pl.ds(pl.multiple_of(me * width, 128), width)
    barrier = pltpu.get_barrier_semaphore()
    pl.semaphore_signal(barrier, inc=1, device_id=other, device_id_type=pl.DeviceIdType.MESH)
    pl.semaphore_wait(barrier, 1)
    away = pltpu.make_async_remote_copy(
        src_ref=mine_ref,
        dst_ref=full_ref.at[:, columns],
        send_sem=send_sem,
        recv_sem=recv_sem,
        device_id=other,
        device_id_type=pl.DeviceIdType.MESH,
    )
    away.start()
    own = pltpu.make_async_copy(mine_ref, full_ref.at[:, columns], own_sem)
    own.start()
    own.wait()
    away.wait()


def both_halves(mine):
    rows, width = mine.shape
    vmem = pl.BlockSpec(memory_space=pltpu.VMEM)
    return pl.pallas_call(
        exchange_kernel,
        out_shape=jax.ShapeDtypeStruct((rows, 2 * width), mine.dtype),
        in_specs=[vmem],
        out_specs=vmem,
        scratch_shapes=[pltpu.SemaphoreType.DMA] * 3,
        compiler_params=pltpu.CompilerParams(
            collective_id=3, has_side_effects=True, vmem_limit_bytes=12 * 1024 * 1024
        ),
        cost_estimate=pl.CostEstimate(
            flops=0, bytes_accessed=6 * rows * width, transcendentals=0
        ),
    )(mine)


def on_device(
    frames,
    norm_gain,
    norm_bias,
    input_weight,
    depth_weight,
    batch_scale,
    batch_shift,
    output_weight,
    upstream,
    replica_blocks,
    segment,
):
    replicas = lax.axis_size("dp")
    my_index = lax.axis_index("dp")
    tensor_index = lax.axis_index("tensor")
    full_width = norm_gain.shape[0]
    load_rows, part_width = frames.shape
    row_count = segment.shape[0]
    rows_part = upstream.shape[0]
    load_blocks = load_rows // BLK
    cap_blocks = row_count // BLK
    per_peer = cdiv(cap_blocks, replicas)
    row_start = tensor_index * rows_part
    column_start = tensor_index * part_width

    run_ends = jnp.cumsum(replica_blocks)
    starts = run_ends - replica_blocks
    peers = jnp.arange(replicas, dtype=jnp.int32)
    is_mine = peers == my_index
    my_start = jnp.sum(jnp.where(is_mine, starts, 0))
    my_blocks = jnp.sum(jnp.where(is_mine, replica_blocks, 0))
    my_end = my_start + my_blocks
    bucket = jnp.arange(per_peer, dtype=jnp.int32)
    first_out = cdiv(jnp.maximum(starts - my_index, 0), replicas)
    send_block = jnp.minimum(first_out[:, None] + bucket[None, :], load_blocks - 1)
    skipped = cdiv(jnp.maximum(my_start - peers, 0), replicas)
    arriving = peers[:, None] + replicas * (skipped[:, None] + bucket[None, :])
    landing = jnp.clip(arriving - my_start, 0, cap_blocks - 1)
    slots = jnp.arange(cap_blocks, dtype=jnp.int32)
    slot_number = my_start + slots
    slot_source = slot_number % replicas
    slot_skipped = cdiv(jnp.maximum(my_start - slot_source, 0), replicas)
    slot_pos = jnp.clip(slot_number // replicas - slot_skipped, 0, per_peer - 1)
    pick_in = slot_source * per_peer + slot_pos
    load_numbers = my_index + replicas * jnp.arange(load_blocks, dtype=jnp.int32)
    target = jnp.sum((run_ends[None, :] <= load_numbers[:, None]).astype(jnp.int32), axis=1)
    target_start = jnp.sum(jnp.where(peers[None, :] == target[:, None], starts[None, :], 0), axis=1)
    slot_out = jnp.arange(load_blocks, dtype=jnp.int32) - cdiv(
        jnp.maximum(target_start - my_index, 0), replicas
    )
    pick_back = target * per_peer + slot_out

    active = slots < my_blocks
    active_rows = jnp.repeat(active, BLK)
    active_mine = lax.dynamic_slice_in_dim(active_rows, row_start, rows_part)[:, None]

    upstream_whole = lax.all_gather(upstream, "tensor", axis=0, tiled=True)
    delta_whole = jnp.where(active_rows[:, None], upstream_whole, jnp.zeros_like(upstream_whole))

    outbox = frames.reshape(load_blocks, BLK, part_width)[send_block.reshape(-1)]
    arrived = lax.all_to_all(
        outbox.reshape(replicas, per_peer, BLK, part_width),
        "dp",
        split_axis=0,
        concat_axis=0,
        tiled=True,
    )
    packed = jnp.where(
        active[:, None, None],
        arrived.reshape(replicas * per_peer, BLK, part_width)[pick_in],
        jnp.zeros((), jnp.bfloat16),
    )
    local_rows = packed.reshape(row_count, part_width)
    if lax.axis_size("tensor") == 2 and part_width % 128 == 0 and row_count % 64 == 0:
        gathered = both_halves(local_rows)
    else:
        gathered = lax.all_gather(local_rows, "tensor", axis=1, tiled=True)

    delta_swish = lax.dot_general(
        delta_whole, output_weight, (((1,), (1,)), ((), ())), preferred_element_type=jnp.float32
    )

    gathered_float = gathered.astype(jnp.float32)
    center = jnp.mean(gathered_float, axis=1, keepdims=True)
    spread = jnp.mean(jnp.square(gathered_float - center), axis=1, keepdims=True)
    scale_row = lax.rsqrt(spread + epsilon)
    standard_full = (gathered_float - center) * scale_row
    normed = (standard_full * norm_gain + norm_bias).astype(jnp.bfloat16)
    projected = jnp.einsum("td,kcd->ktc", normed, input_weight, preferred_element_type=jnp.float32)

    swish, delta_linear, delta_gate, tap_local = conv_both(
        projected, delta_swish, segment, active_rows, depth_weight, batch_scale, batch_shift
    )

    back_term = (
        jnp.dot(delta_linear, input_weight[0], preferred_element_type=jnp.float32)
        + jnp.dot(delta_gate, input_weight[1], preferred_element_type=jnp.float32)
    ).astype(jnp.bfloat16)
    back_term, swish, delta_linear, delta_gate = lax.optimization_barrier(
        (back_term, swish, delta_linear, delta_gate)
    )
    delta_normed = lax.psum_scatter(back_term, "tensor", scatter_dimension=1, tiled=True).astype(
        jnp.float32
    )
    mixed_term = jnp.dot(swish, output_weight, preferred_element_type=jnp.float32).astype(
        jnp.bfloat16
    )
    mixed_sum = lax.psum_scatter(
        mixed_term, "tensor", scatter_dimension=0, tiled=True
    ).astype(jnp.float32)
    back_float = back_term.astype(jnp.float32) * norm_gain
    unit_local = jnp.sum(back_float, axis=1)
    cross_local = jnp.sum(back_float * standard_full, axis=1)
    unit_total, cross_total = lax.psum((unit_local, cross_local), "tensor")

    def over_rows(left, right):
        return lax.dot_general(
            left, right, (((0,), (0,)), ((), ())), preferred_element_type=jnp.float32
        ).astype(jnp.bfloat16)

    by_kernel = (
        part_width % (16 * replicas) == 0 and replicas & (replicas - 1) == 0 and replicas > 2
    )
    terms = (
        over_rows(delta_linear, normed),
        over_rows(delta_gate, normed),
        over_rows(swish, delta_whole),
    )

    residual_part = lax.dynamic_slice_in_dim(gathered, row_start, rows_part, 0)
    block_output = jnp.where(
        active_mine, residual_part.astype(jnp.float32) + mixed_sum, 0.0
    ).astype(jnp.bfloat16)

    gain_part = lax.dynamic_slice_in_dim(norm_gain, column_start, part_width)
    standard = (local_rows.astype(jnp.float32) - center) * scale_row
    delta_part = lax.dynamic_slice_in_dim(delta_whole, column_start, part_width, 1)
    delta_rows = delta_part.astype(jnp.float32) + scale_row * (
        delta_normed * gain_part
        - (unit_total / full_width)[:, None]
        - standard * (cross_total / full_width)[:, None]
    )
    delta_blocks = delta_rows.astype(jnp.bfloat16).reshape(cap_blocks, BLK, part_width)
    homebound = delta_blocks[landing.reshape(-1)].reshape(replicas, per_peer, BLK, part_width)

    taps = depth_weight.shape[0]
    norm_local = jnp.stack([jnp.sum(delta_normed * standard, axis=0), jnp.sum(delta_normed, axis=0)])
    small = jnp.concatenate([tap_local, norm_local])
    homebound, terms, small = lax.optimization_barrier((homebound, terms, small))
    if by_kernel:
        summed, small_summed = sum_over_dp(terms, replicas, 1, small)
    else:
        summed, small_summed = lax.psum((jnp.stack(terms), small), "dp")
    weight_summed, out_summed = summed[:2], summed[2]
    returned = lax.all_to_all(homebound, "dp", split_axis=0, concat_axis=0, tiled=True)
    frame_gradient = returned.reshape(replicas * per_peer, BLK, part_width)[pick_back].reshape(
        load_rows, part_width
    )
    return (
        block_output,
        frame_gradient,
        weight_summed,
        out_summed,
        small_summed[:taps],
        small_summed[taps],
        small_summed[taps + 1],
    )


def solution(mesh):
    in_specs = (
        P("dp", "tensor"),
        P(),
        P(),
        P(None, "tensor", None),
        P(None, "tensor"),
        P("tensor"),
        P("tensor"),
        P("tensor", None),
        P(("dp", "tensor"), None),
        P(),
        P("dp"),
    )
    out_specs = (
        P(("dp", "tensor"), None),
        P("dp", "tensor"),
        P(None, "tensor", None),
        P("tensor", None),
        P(None, "tensor"),
        P("tensor"),
        P("tensor"),
    )
    return jax.shard_map(
        on_device, mesh=mesh, in_specs=in_specs, out_specs=out_specs, check_vma=False
    )
```

```python
import functools

import jax
import jax.numpy as jnp
from jax import lax
from jax.experimental import pallas as pl
from jax.experimental.pallas import tpu as pltpu
from jax.sharding import PartitionSpec as P

BLK = 8


epsilon = 1e-05


def cdiv(a, b):
    return (a + b - 1) // b


def conv_kernel(
    taps,
    front,
    tile,
    linear_ref,
    gate_ref,
    delta_ref,
    seg_ref,
    active_ref,
    weight_ref,
    scale_ref,
    shift_ref,
    swish_ref,
    dlin_ref,
    dgate_ref,
    tap_ref,
    glu_pad,
    conv_pad,
    seg_pad,
    tap_acc,
):
    rows, width = linear_ref.shape
    pad = taps
    padded = rows + 2 * pad

    zeros = jnp.zeros((pad, width), jnp.float32)
    glu_pad[0:pad, :] = zeros
    glu_pad[pad + rows : padded, :] = zeros
    conv_pad[0:pad, :] = zeros
    conv_pad[pad + rows : padded, :] = zeros

    @pl.when(pl.program_id(0) == 0)
    def _():
        outside = jnp.full((pad, width), -1, jnp.int32)
        seg_pad[0:pad, :] = outside
        seg_pad[pad + rows : padded, :] = outside
        seg_pad[pad : pad + rows, :] = jnp.broadcast_to(seg_ref[...], (rows, width))

    tap_acc[...] = jnp.zeros_like(tap_acc)

    for start in range(0, rows, tile):
        part = pl.ds(start, tile)
        glu = linear_ref[part, :] * jax.nn.sigmoid(gate_ref[part, :])
        glu = glu.astype(jnp.bfloat16).astype(jnp.float32)
        glu_pad[pl.ds(pad + start, tile), :] = jnp.where(active_ref[part, :] > 0, glu, 0.0)

    @pl.loop(0, rows // tile)
    def _(step):
        start = pl.multiple_of(step * tile, tile)
        part = pl.ds(start, tile)
        own = seg_pad[pl.ds(pad + start, tile), :]
        total = jnp.zeros((tile, width), jnp.float32)
        for j in range(taps):
            near = pl.ds(start + (pad + j - front), tile)
            picked = jnp.where(seg_pad[near, :] == own, glu_pad[near, :], 0.0)
            total = total + weight_ref[j : j + 1, :] * picked
        scale = scale_ref[...]
        preswish = total * scale + shift_ref[...]
        pre_sigmoid = jax.nn.sigmoid(preswish)
        swish_ref[part, :] = (preswish * pre_sigmoid).astype(jnp.bfloat16)
        conv_pad[pl.ds(pad + start, tile), :] = (
            delta_ref[part, :]
            * pre_sigmoid
            * (1.0 + preswish * (1.0 - pre_sigmoid))
            * scale
        )

    @pl.loop(0, rows // tile)
    def _(step):
        start = pl.multiple_of(step * tile, tile)
        part = pl.ds(start, tile)
        own = seg_pad[pl.ds(pad + start, tile), :]
        glu = glu_pad[pl.ds(pad + start, tile), :]
        total = jnp.zeros((tile, width), jnp.float32)
        for j in range(taps):
            near = pl.ds(start + (pad + front - j), tile)
            picked = jnp.where(seg_pad[near, :] == own, conv_pad[near, :], 0.0)
            total = total + weight_ref[j : j + 1, :] * picked
            product = (glu * picked).reshape(tile // 8, 8, width)
            tap_acc[j] = tap_acc[j] + jnp.sum(product, axis=0)
        total = jnp.where(active_ref[part, :] > 0, total, 0.0)
        gate_sigmoid = jax.nn.sigmoid(gate_ref[part, :])
        dlin = total * gate_sigmoid
        dlin_ref[part, :] = dlin.astype(jnp.bfloat16)
        dgate_ref[part, :] = (dlin * linear_ref[part, :] * (1.0 - gate_sigmoid)).astype(
            jnp.bfloat16
        )

    tap_ref[...] = jnp.sum(tap_acc[...], axis=1)


def conv_both(projected, delta_swish, segment, active, weight, scale, shift):
    _, rows, given = projected.shape
    taps = weight.shape[0]
    width = 128
    channels = cdiv(given, width) * width

    def widen(array):
        extra = channels - given
        return jnp.pad(array, [(0, 0)] * (array.ndim - 1) + [(0, extra)]) if extra else array

    projected, delta_swish, weight = widen(projected), widen(delta_swish), widen(weight)
    scale, shift = widen(scale), widen(shift)
    tile = min(64, rows)
    padded = rows + 2 * taps
    column = pl.BlockSpec((rows, width), lambda c: (0, c))
    half = lambda h: pl.BlockSpec((None, rows, width), lambda c: (h, 0, c))
    row = pl.BlockSpec((1, width), lambda c: (0, c))
    whole = pl.BlockSpec((rows, 1), lambda c: (0, 0))
    results = pl.pallas_call(
        functools.partial(conv_kernel, taps, taps // 2, tile),
        grid=(channels // width,),
        out_shape=(
            jax.ShapeDtypeStruct((rows, channels), jnp.bfloat16),
            jax.ShapeDtypeStruct((rows, channels), jnp.bfloat16),
            jax.ShapeDtypeStruct((rows, channels), jnp.bfloat16),
            jax.ShapeDtypeStruct((taps, channels), jnp.float32),
        ),
        in_specs=[
            half(0),
            half(1),
            column,
            whole,
            whole,
            pl.BlockSpec((taps, width), lambda c: (0, c)),
            row,
            row,
        ],
        out_specs=[column, column, column, pl.BlockSpec((taps, width), lambda c: (0, c))],
        scratch_shapes=[
            pltpu.VMEM((padded, width), jnp.float32),
            pltpu.VMEM((padded, width), jnp.float32),
            pltpu.VMEM((padded, width), jnp.int32),
            pltpu.VMEM((taps, 8, width), jnp.float32),
        ],
        compiler_params=pltpu.CompilerParams(vmem_limit_bytes=24 * 1024 * 1024),
        cost_estimate=pl.CostEstimate(
            flops=10 * rows * channels * taps,
            bytes_accessed=18 * rows * channels,
            transcendentals=3 * rows * channels,
        ),
    )(
        projected,
        projected,
        delta_swish,
        segment[:, None],
        active.astype(jnp.int32)[:, None],
        weight,
        scale[None, :],
        shift[None, :],
    )
    return [result[:, :given] for result in results] if channels != given else results


def sum_kernel(chunk, per_array, orders, with_small, *refs):
    arrays = len(per_array)
    bits = len(orders[0])
    ins, refs = refs[:arrays], refs[arrays:]
    if with_small:
        small_in, stacked_out, last_out, small_out = refs[:4]
        red, got, first, loads, sends, recvs = refs[4:10]
        small_buf, small_got, small_sends, small_recvs = refs[10:]
    else:
        stacked_out, last_out, red, got, first, loads, sends, recvs = refs
    me = lax.axis_index("dp")
    digit = [(me // (1 << b)) % 2 for b in range(bits)]
    partner = [me + (1 - 2 * digit[b]) * (1 << b) for b in range(bits)]
    places = [(a, i * chunk) for a in range(arrays) for i in range(per_array[a])]
    chunks = range(len(places))
    lengths = [chunk >> (s + 1) for s in range(bits)]
    bases = [chunk - 2 * lengths[s] for s in range(bits)]

    def target(c, start, size):
        a, top = places[c]
        rows = pl.ds(pl.multiple_of(top + start, 16), size)
        return stacked_out.at[a, rows] if a < arrays - 1 else last_out.at[rows]

    def held(c, s, start, size):
        if s == 0:
            a, top = places[c]
            return ins[a].at[pl.ds(pl.multiple_of(top + start, 16), size)]
        return red.at[c, pl.ds(pl.multiple_of(bases[s - 1] + start, 16), size)]

    def halving(c, s):
        b = orders[c][s]
        return pltpu.make_async_remote_copy(
            src_ref=held(c, s, (1 - digit[b]) * lengths[s], lengths[s]),
            dst_ref=got.at[c, pl.ds(bases[s], lengths[s])],
            send_sem=sends.at[s, c],
            recv_sem=recvs.at[s, c],
            device_id={"dp": partner[b]},
            device_id_type=pl.DeviceIdType.MESH,
        )

    def load(c):
        b = orders[c][0]
        return pltpu.make_async_copy(
            held(c, 0, digit[b] * lengths[0], lengths[0]), first.at[c], loads.at[c]
        )

    def offset(c, s):
        return sum(digit[orders[c][k]] * lengths[k] for k in range(s + 1))

    def doubling(c, s):
        b = orders[c][s]
        place = target(c, offset(c, s), lengths[s])
        return pltpu.make_async_remote_copy(
            src_ref=place,
            dst_ref=place,
            send_sem=sends.at[bits + s, c],
            recv_sem=recvs.at[bits + s, c],
            device_id={"dp": partner[b]},
            device_id_type=pl.DeviceIdType.MESH,
        )

    def small_copy(s):
        return pltpu.make_async_remote_copy(
            src_ref=small_buf.at[s],
            dst_ref=small_got.at[s],
            send_sem=small_sends.at[s],
            recv_sem=small_recvs.at[s],
            device_id={"dp": partner[s]},
            device_id_type=pl.DeviceIdType.MESH,
        )

    barrier = pltpu.get_barrier_semaphore()
    for b in range(bits):
        pl.semaphore_signal(
            barrier, inc=1, device_id={"dp": partner[b]}, device_id_type=pl.DeviceIdType.MESH
        )
    pl.semaphore_wait(barrier, bits)

    if with_small:
        small_buf[0] = small_in[...]
        small_copy(0).start()
    for c in chunks:
        halving(c, 0).start()
    for c in chunks:
        load(c).start()

    def halving_done(c, s):
        halving(c, s).wait_recv()
        if s == 0:
            load(c).wait()
            kept = first.at[c]
        else:
            kept = held(c, s, digit[orders[c][s]] * lengths[s], lengths[s])
        come = got.at[c, pl.ds(bases[s], lengths[s])]
        if s < bits - 1:
            into = red.at[c, pl.ds(bases[s], lengths[s])]
        else:
            into = target(c, offset(c, s), lengths[s])

        @pl.loop(0, lengths[s] // 16)
        def _(i):
            rows = pl.ds(pl.multiple_of(i * 16, 16), 16)
            into[rows, :] = (
                kept[rows, :].astype(jnp.float32) + come[rows, :].astype(jnp.float32)
            ).astype(jnp.bfloat16)

        if s < bits - 1:
            halving(c, s + 1).start()
        else:
            doubling(c, s).start()

    def doubling_done(c, s):
        doubling(c, s).wait_recv()
        if s > 0:
            doubling(c, s - 1).start()

    def small_done(s):
        small_copy(s).wait_recv()
        total = small_buf[s] + small_got[s]
        if s < bits - 1:
            small_buf[s + 1] = total
            small_copy(s + 1).start()
        else:
            small_out[...] = total

    events = [(c + 2 * k, k, c) for c in chunks for k in range(2 * bits)]
    for _, k, c in sorted(events):
        if k < bits:
            halving_done(c, k)
            if with_small and c == 0:
                small_done(k)
        else:
            doubling_done(c, 2 * bits - 1 - k)
    for s in range(bits):
        if with_small:
            small_copy(s).wait_send()
        for c in chunks:
            halving(c, s).wait_send()
            doubling(c, s).wait_send()


def sum_over_dp(terms, n, collective_id, small=None):
    rows, width = terms[0].shape
    bits = n.bit_length() - 1
    chunk = 16 * n
    per_array = [rows // chunk] * len(terms)
    count = sum(per_array)
    plain = list(range(bits))
    turned = [0] + plain[2:] + [1]
    orders = [turned if c == 0 else plain for c in range(count)]
    vmem = pl.BlockSpec(memory_space=pltpu.VMEM)
    with_small = small is not None
    extra = (small,) if with_small else ()
    small_shapes = [pltpu.VMEM((bits,) + e.shape, jnp.float32) for e in extra * 2]
    small_semaphores = [pltpu.SemaphoreType.DMA((bits,)) for e in extra * 2]
    return pl.pallas_call(
        functools.partial(sum_kernel, chunk, per_array, orders, with_small),
        out_shape=[
            jax.ShapeDtypeStruct((len(terms) - 1, rows, width), jnp.bfloat16),
            jax.ShapeDtypeStruct((rows, width), jnp.bfloat16),
        ]
        + [jax.ShapeDtypeStruct(e.shape, jnp.float32) for e in extra],
        in_specs=[pl.BlockSpec(memory_space=pl.ANY)] * len(terms) + [vmem] * len(extra),
        out_specs=[vmem] * (2 + len(extra)),
        scratch_shapes=[
            pltpu.VMEM((count, chunk, width), jnp.bfloat16),
            pltpu.VMEM((count, chunk, width), jnp.bfloat16),
            pltpu.VMEM((count, chunk // 2, width), jnp.bfloat16),
            pltpu.SemaphoreType.DMA((count,)),
            pltpu.SemaphoreType.DMA((2 * bits, count)),
            pltpu.SemaphoreType.DMA((2 * bits, count)),
        ]
        + small_shapes
        + small_semaphores,
        compiler_params=pltpu.CompilerParams(
            collective_id=collective_id, has_side_effects=True, vmem_limit_bytes=44 * 1024 * 1024
        ),
        cost_estimate=pl.CostEstimate(
            flops=count * chunk * width,
            bytes_accessed=4 * count * chunk * width,
            transcendentals=0,
        ),
    )(*terms, *extra)


def exchange_kernel(mine_ref, full_ref, own_sem, send_sem, recv_sem):
    width = mine_ref.shape[1]
    me = lax.axis_index("tensor")
    other = {"tensor": 1 - me}
    columns = pl.ds(pl.multiple_of(me * width, 128), width)
    barrier = pltpu.get_barrier_semaphore()
    pl.semaphore_signal(barrier, inc=1, device_id=other, device_id_type=pl.DeviceIdType.MESH)
    pl.semaphore_wait(barrier, 1)
    away = pltpu.make_async_remote_copy(
        src_ref=mine_ref,
        dst_ref=full_ref.at[:, columns],
        send_sem=send_sem,
        recv_sem=recv_sem,
        device_id=other,
        device_id_type=pl.DeviceIdType.MESH,
    )
    away.start()
    own = pltpu.make_async_copy(mine_ref, full_ref.at[:, columns], own_sem)
    own.start()
    own.wait()
    away.wait()


def both_halves(mine):
    rows, width = mine.shape
    vmem = pl.BlockSpec(memory_space=pltpu.VMEM)
    return pl.pallas_call(
        exchange_kernel,
        out_shape=jax.ShapeDtypeStruct((rows, 2 * width), mine.dtype),
        in_specs=[vmem],
        out_specs=vmem,
        scratch_shapes=[pltpu.SemaphoreType.DMA] * 3,
        compiler_params=pltpu.CompilerParams(
            collective_id=3, has_side_effects=True, vmem_limit_bytes=12 * 1024 * 1024
        ),
        cost_estimate=pl.CostEstimate(
            flops=0, bytes_accessed=6 * rows * width, transcendentals=0
        ),
    )(mine)


def on_device(
    frames,
    norm_gain,
    norm_bias,
    input_weight,
    depth_weight,
    batch_scale,
    batch_shift,
    output_weight,
    upstream,
    replica_blocks,
    segment,
):
    replicas = lax.axis_size("dp")
    my_index = lax.axis_index("dp")
    tensor_index = lax.axis_index("tensor")
    full_width = norm_gain.shape[0]
    load_rows, part_width = frames.shape
    row_count = segment.shape[0]
    rows_part = upstream.shape[0]
    load_blocks = load_rows // BLK
    cap_blocks = row_count // BLK
    per_peer = cdiv(cap_blocks, replicas)
    row_start = tensor_index * rows_part
    column_start = tensor_index * part_width

    run_ends = jnp.cumsum(replica_blocks)
    starts = run_ends - replica_blocks
    peers = jnp.arange(replicas, dtype=jnp.int32)
    is_mine = peers == my_index
    my_start = jnp.sum(jnp.where(is_mine, starts, 0))
    my_blocks = jnp.sum(jnp.where(is_mine, replica_blocks, 0))
    my_end = my_start + my_blocks
    bucket = jnp.arange(per_peer, dtype=jnp.int32)
    first_out = cdiv(jnp.maximum(starts - my_index, 0), replicas)
    send_block = jnp.minimum(first_out[:, None] + bucket[None, :], load_blocks - 1)
    skipped = cdiv(jnp.maximum(my_start - peers, 0), replicas)
    arriving = peers[:, None] + replicas * (skipped[:, None] + bucket[None, :])
    landing = jnp.clip(arriving - my_start, 0, cap_blocks - 1)
    slots = jnp.arange(cap_blocks, dtype=jnp.int32)
    slot_number = my_start + slots
    slot_source = slot_number % replicas
    slot_skipped = cdiv(jnp.maximum(my_start - slot_source, 0), replicas)
    slot_pos = jnp.clip(slot_number // replicas - slot_skipped, 0, per_peer - 1)
    pick_in = slot_source * per_peer + slot_pos
    load_numbers = my_index + replicas * jnp.arange(load_blocks, dtype=jnp.int32)
    target = jnp.sum((run_ends[None, :] <= load_numbers[:, None]).astype(jnp.int32), axis=1)
    target_start = jnp.sum(jnp.where(peers[None, :] == target[:, None], starts[None, :], 0), axis=1)
    slot_out = jnp.arange(load_blocks, dtype=jnp.int32) - cdiv(
        jnp.maximum(target_start - my_index, 0), replicas
    )
    pick_back = target * per_peer + slot_out

    active = slots < my_blocks
    active_rows = jnp.repeat(active, BLK)
    active_mine = lax.dynamic_slice_in_dim(active_rows, row_start, rows_part)[:, None]

    upstream_whole = lax.all_gather(upstream, "tensor", axis=0, tiled=True)
    delta_whole = jnp.where(active_rows[:, None], upstream_whole, jnp.zeros_like(upstream_whole))

    outbox = frames.reshape(load_blocks, BLK, part_width)[send_block.reshape(-1)]
    arrived = lax.all_to_all(
        outbox.reshape(replicas, per_peer, BLK, part_width),
        "dp",
        split_axis=0,
        concat_axis=0,
        tiled=True,
    )
    packed = jnp.where(
        active[:, None, None],
        arrived.reshape(replicas * per_peer, BLK, part_width)[pick_in],
        jnp.zeros((), jnp.bfloat16),
    )
    local_rows = packed.reshape(row_count, part_width)
    if lax.axis_size("tensor") == 2 and part_width % 128 == 0 and row_count % 64 == 0:
        gathered = both_halves(local_rows)
    else:
        gathered = lax.all_gather(local_rows, "tensor", axis=1, tiled=True)

    delta_swish = lax.dot_general(
        delta_whole, output_weight, (((1,), (1,)), ((), ())), preferred_element_type=jnp.float32
    )

    gathered_float = gathered.astype(jnp.float32)
    center = jnp.mean(gathered_float, axis=1, keepdims=True)
    spread = jnp.mean(jnp.square(gathered_float - center), axis=1, keepdims=True)
    scale_row = lax.rsqrt(spread + epsilon)
    standard_full = (gathered_float - center) * scale_row
    normed = (standard_full * norm_gain + norm_bias).astype(jnp.bfloat16)
    projected = jnp.einsum("td,kcd->ktc", normed, input_weight, preferred_element_type=jnp.float32)

    swish, delta_linear, delta_gate, tap_local = conv_both(
        projected, delta_swish, segment, active_rows, depth_weight, batch_scale, batch_shift
    )

    back_term = (
        jnp.dot(delta_linear, input_weight[0], preferred_element_type=jnp.float32)
        + jnp.dot(delta_gate, input_weight[1], preferred_element_type=jnp.float32)
    ).astype(jnp.bfloat16)
    back_term, swish, delta_linear, delta_gate = lax.optimization_barrier(
        (back_term, swish, delta_linear, delta_gate)
    )
    delta_normed = lax.psum_scatter(back_term, "tensor", scatter_dimension=1, tiled=True).astype(
        jnp.float32
    )
    mixed_term = jnp.dot(swish, output_weight, preferred_element_type=jnp.float32).astype(
        jnp.bfloat16
    )
    mixed_sum = lax.psum_scatter(
        mixed_term, "tensor", scatter_dimension=0, tiled=True
    ).astype(jnp.float32)
    back_float = back_term.astype(jnp.float32) * norm_gain
    unit_local = jnp.sum(back_float, axis=1)
    cross_local = jnp.sum(back_float * standard_full, axis=1)
    unit_total, cross_total = lax.psum((unit_local, cross_local), "tensor")

    def over_rows(left, right):
        return lax.dot_general(
            left, right, (((0,), (0,)), ((), ())), preferred_element_type=jnp.float32
        ).astype(jnp.bfloat16)

    by_kernel = (
        part_width % (16 * replicas) == 0 and replicas & (replicas - 1) == 0 and replicas > 2
    )
    terms = (
        over_rows(delta_linear, normed),
        over_rows(delta_gate, normed),
        over_rows(swish, delta_whole),
    )

    residual_part = lax.dynamic_slice_in_dim(gathered, row_start, rows_part, 0)
    block_output = jnp.where(
        active_mine, residual_part.astype(jnp.float32) + mixed_sum, 0.0
    ).astype(jnp.bfloat16)

    gain_part = lax.dynamic_slice_in_dim(norm_gain, column_start, part_width)
    standard = (local_rows.astype(jnp.float32) - center) * scale_row
    delta_part = lax.dynamic_slice_in_dim(delta_whole, column_start, part_width, 1)
    delta_rows = delta_part.astype(jnp.float32) + scale_row * (
        delta_normed * gain_part
        - (unit_total / full_width)[:, None]
        - standard * (cross_total / full_width)[:, None]
    )
    delta_blocks = delta_rows.astype(jnp.bfloat16).reshape(cap_blocks, BLK, part_width)
    homebound = delta_blocks[landing.reshape(-1)].reshape(replicas, per_peer, BLK, part_width)

    taps = depth_weight.shape[0]
    norm_local = jnp.stack([jnp.sum(delta_normed * standard, axis=0), jnp.sum(delta_normed, axis=0)])
    small = jnp.concatenate([tap_local, norm_local])
    homebound, terms, small = lax.optimization_barrier((homebound, terms, small))
    if by_kernel:
        weight_summed, out_summed, small_summed = sum_over_dp(terms, replicas, 1, small)
    else:
        weight_summed, out_summed, small_summed = lax.psum(
            (jnp.stack(terms[:2]), terms[2], small), "dp"
        )
    returned = lax.all_to_all(homebound, "dp", split_axis=0, concat_axis=0, tiled=True)
    frame_gradient = returned.reshape(replicas * per_peer, BLK, part_width)[pick_back].reshape(
        load_rows, part_width
    )
    return (
        block_output,
        frame_gradient,
        weight_summed,
        out_summed,
        small_summed[:taps],
        small_summed[taps],
        small_summed[taps + 1],
    )


def solution(mesh):
    in_specs = (
        P("dp", "tensor"),
        P(),
        P(),
        P(None, "tensor", None),
        P(None, "tensor"),
        P("tensor"),
        P("tensor"),
        P("tensor", None),
        P(("dp", "tensor"), None),
        P(),
        P("dp"),
    )
    out_specs = (
        P(("dp", "tensor"), None),
        P("dp", "tensor"),
        P(None, "tensor", None),
        P("tensor", None),
        P(None, "tensor"),
        P("tensor"),
        P("tensor"),
    )
    return jax.shard_map(
        on_device, mesh=mesh, in_specs=in_specs, out_specs=out_specs, check_vma=False
    )
```
